32 devices in a mesh: groups: 2 (over x), chan: 16 (over z, y, core).
Axes of the slice: x: 2, y: 2, z: 4, core: 2. Of those that a mesh axis runs over, the one named last changes fastest.
Arguments:
- records: bfloat16 [256, 32, 2048], P(('groups', 'chan')), parts along dimension 0, may hold values from -6 to 6
- window_valid: float32 [256, 32], P(('groups', 'chan')), parts along dimension 0, may hold values from 0 to 1, as said below
- band_low: int32 [256], P(('groups', 'chan')), parts along dimension 0, may hold values from 0 to 255
- band_high: int32 [256], P(('groups', 'chan')), parts along dimension 0, may hold values from 768 to 1024
- pair_counts: int32 [32], P('groups'), parts along dimension 0, may hold values from 1 to 4, 32 in all
- partners: int32 [32, 4], P('groups'), parts along dimension 0, may hold values from 0 to 15
Outputs:
- stacks: bfloat16 [32, 4, 1024, 128], P(('groups', 'chan')), parts along dimension 0
The draws below stay inside these ranges and needn't reach their ends.
There are 2 independent parts, one for each index of `groups`. The reference program is written for one: setup_inputs(seed, part) draws one part's arguments, and reference() takes and returns one part's arrays. A program takes and returns all parts, laid end to end along the dimension named above; each array names one. Nothing has to cross between parts.
Inputs may be any that keep to these rules, and one draw needn't show every extreme that they name: `window_valid`: 0 marks a window without data; some channels have no window with data. `pair_counts`: the counts sum to 32, and the largest is 4.
All inputs are finite; a program needn't handle non-finite values.
Results may differ from the reference program's by a relative error of at most 0.0065.
Values may be sent and summed in bfloat16 or wider, within the bound.
A program may use at most 128 MiB of HBM per device.

```python
import math
import jax
import jax.numpy as jnp
import numpy as np
from jax import lax

F = 1024
L = 2048
CH_DEV = 8
W = 32
P_MAX = 4
SMOOTH = 8
C = 128
N_CHAN = 16


def draw_window_valid(key, part):
    dead_key, window_key, level_key = jax.random.split(jax.random.fold_in(key, 11), 3)
    alive = jax.random.randint(dead_key, (C, 1), 0, 8) > 0
    holding = jax.random.randint(window_key, (C, W), 0, 4) > 0
    level = jnp.exp(jax.random.uniform(level_key, (C, W), jnp.float32, math.log(0.1), 0.0))
    return jnp.where(alive & holding, level, 0.0).astype(jnp.float32)


def with_ends(entries, own_key, low, largest):
    longest = entries.shape.index(max(entries.shape))
    spots = []
    for shift in (0, 1):
        where = [jax.random.randint(jax.random.fold_in(own_key, axis), (), 0, length) for axis, length in enumerate(entries.shape)]
        where[longest] = (where[longest] + shift) % entries.shape[longest]
        spots.append(tuple(where))
    return entries.at[spots[0]].set(low).at[spots[1]].set(largest)


def levels(own_key, shape, shards, smallest, top_value):
    def one(dim, parts):
        heights = jax.random.uniform(jax.random.fold_in(jax.random.fold_in(own_key, 6), dim), (parts,), jnp.float32, smallest / len(shards), top_value / len(shards))
        return jnp.repeat(jnp.exp(heights), shape[dim] // parts).reshape((-1,) + (1,) * (len(shape) - dim - 1))

    gain = one(*shards[0])
    for cut in shards[1:]:
        gain = gain * one(*cut)
    return gain


def length_profile(amount, total, most, slope):
    portions = [(1 << 20) // math.isqrt(grade ** slope) + 1 for grade in range(2, amount + 1)]
    rest, given = total - most - (amount - 1), [1] * (amount - 1)
    while rest > 0:
        movable = [i for i in range(amount - 1) if given[i] < most]
        whole, budget = sum([portions[i] for i in movable]), rest
        for i in movable:
            extra = min(most - given[i], max(1, budget * portions[i] // whole), rest)
            given[i] = given[i] + extra
            rest = rest - extra
    return np.array([most] + given)


def uneven(key, count, total, limit, slope):
    if count == 2:
        one = jax.random.randint(key, (), max(1, total - limit), min(limit, total - 1) + 1)
        return jnp.stack([one, total - one])
    lengths = jnp.asarray(length_profile(count, total, limit, slope), jnp.int32)
    couples = (count - 1) // 2
    giver, taker = lengths[1:1 + 2 * couples:2], lengths[2:2 + 2 * couples:2]
    margin = jnp.minimum(giver - 1, limit - taker)
    shifted = jax.random.randint(jax.random.fold_in(key, 1), (couples,), 0, 1 << 20) % (margin + 1)
    lengths = lengths.at[1:1 + 2 * couples:2].set(giver - shifted).at[2:2 + 2 * couples:2].set(taker + shifted)
    return lengths[jax.random.permutation(jax.random.fold_in(key, 2), count)]


def noise(rng, dims, spread, reach, pieces=(), kind=jnp.bfloat16):
    array = jax.random.normal(rng, dims, jnp.float32) * spread
    if len(pieces) > 0:
        array = levels(rng, dims, pieces, -0.22, 0.18) * array
    return jnp.clip(array, min=-reach, max=reach).astype(kind)


def setup_inputs(seed: int = 0, part: int = 0) -> dict:
    arg_keys = jax.random.split(jax.random.key(seed), 7)
    part_keys = jax.random.split(jax.random.fold_in(arg_keys[6], part), 7)
    return {
        "records": noise(part_keys[0], (C, W, L), 1.0, 6.0, ((0, 16),)),
        "window_valid": draw_window_valid(jax.random.fold_in(jax.random.fold_in(arg_keys[6], part), 71), part),
        "band_low": with_ends(jax.random.randint(part_keys[2], (C,), 0, F // 4), jax.random.fold_in(part_keys[2], 1), 0, (F // 4) - 1).astype(jnp.int32),
        "band_high": with_ends(jax.random.randint(part_keys[3], (C,), 3 * F // 4, F + 1), jax.random.fold_in(part_keys[3], 1), 3 * F // 4, F).astype(jnp.int32),
        "pair_counts": uneven(part_keys[4], N_CHAN, 2 * N_CHAN, P_MAX, 2).astype(jnp.int32),
        "partners": with_ends(jax.random.randint(part_keys[5], (N_CHAN, P_MAX), 0, N_CHAN), jax.random.fold_in(part_keys[5], 1), 0, N_CHAN - 1).astype(jnp.int32),
    }


def dft_table(length, first_bin, bin_count):
    sample_index = lax.broadcasted_iota(jnp.int32, (length, bin_count), 0)
    bin_index = lax.broadcasted_iota(jnp.int32, (length, bin_count), 1) + first_bin
    phase_step = sample_index * bin_index % length
    angles = phase_step.astype(jnp.float32) * (2.0 * math.pi / length)
    return jnp.concatenate([jnp.cos(angles), -jnp.sin(angles)], axis=1).astype(jnp.bfloat16)

def finish(spectrum, band_low, band_high, channels, windows):
    bin_total = spectrum.shape[1]
    magnitude = jnp.sqrt(spectrum[0] * spectrum[0] + spectrum[1] * spectrum[1])
    offsets = lax.broadcasted_iota(jnp.int32, (bin_total, bin_total), 0) - lax.broadcasted_iota(jnp.int32, (bin_total, bin_total), 1)
    window = (jnp.abs(offsets) <= SMOOTH).astype(jnp.float32)
    smoothed = jnp.dot(window, magnitude, precision=lax.Precision.HIGHEST) / lax.optimization_barrier(jnp.sum(window, axis=1, keepdims=True))
    divisor = jnp.maximum(smoothed, 1.0).reshape(bin_total, channels, windows)
    bin_index = lax.broadcasted_iota(jnp.int32, (bin_total, channels, 1), 0)
    inside = ((bin_index >= band_low[None, :, None]) & (bin_index < band_high[None, :, None])).astype(jnp.float32)
    shaped = spectrum.reshape(2, bin_total, channels, windows)
    return (shaped / divisor * inside).astype(jnp.bfloat16).reshape(2, bin_total, channels * windows)

def reference(records, window_valid, band_low, band_high, pair_counts, partners):
    readers = N_CHAN
    length = 2 * F
    dft_full = dft_table(length, 0, F)
    record_blocks = records.reshape(readers, CH_DEV, W, length)
    valid_blocks = window_valid.reshape(readers, CH_DEV, W)
    low_blocks = band_low.reshape(readers, CH_DEV)
    high_blocks = band_high.reshape(readers, CH_DEV)

    def prepare(inputs):
        block_records, block_valid, block_low, block_high = inputs
        one_bit = (jnp.sign(block_records.astype(jnp.float32)) * block_valid.astype(jnp.float32)[:, :, None]).astype(jnp.bfloat16)
        one_bit = one_bit.reshape(CH_DEV * W, length)
        spectrum = lax.dot_general(dft_full, one_bit, (((0,), (1,)), ((), ())), preferred_element_type=jnp.float32)
        spectrum = spectrum.reshape(2, F, CH_DEV * W)
        return finish(spectrum, block_low, block_high, CH_DEV, W)
    whitened = lax.map(prepare, (record_blocks, valid_blocks, low_blocks, high_blocks))
    spectra = whitened.reshape(readers, 2, F, CH_DEV, W)
    valid_all = window_valid.astype(jnp.float32).reshape(readers, CH_DEV, W)

    def one_reader(reader):
        own = spectra[reader].astype(jnp.float32)
        partner_ids = partners[reader]
        others = jnp.take(spectra, partner_ids, axis=0).astype(jnp.float32)
        real_part = jnp.einsum('fim,pfjm->pfij', own[0], others[:, 0]) + jnp.einsum('fim,pfjm->pfij', own[1], others[:, 1])
        imag_part = jnp.einsum('fim,pfjm->pfij', own[1], others[:, 0]) - jnp.einsum('fim,pfjm->pfij', own[0], others[:, 1])
        common = jnp.einsum('im,pjm->pij', valid_all[reader], jnp.take(valid_all, partner_ids, axis=0), precision=lax.Precision.HIGHEST)
        in_use = (jnp.arange(P_MAX, dtype=jnp.int32) < pair_counts[reader]).astype(jnp.float32)
        weight = in_use[:, None, None] / jnp.maximum(common, 1.0)
        both = jnp.stack([real_part, imag_part], axis=2) * weight[:, None, None]
        return both.reshape(P_MAX, F, 2 * CH_DEV * CH_DEV).astype(jnp.bfloat16)
    return lax.map(one_reader, jnp.arange(readers, dtype=jnp.int32))
```

```python
import functools
import math

import jax
import jax.numpy as jnp
import ml_dtypes
import numpy as np
from jax import lax
from jax.experimental import pallas as pl
from jax.experimental.pallas import tpu as pltpu
from jax.sharding import PartitionSpec as P

SMOOTH = 8


def dft_table(length, first_bin, bin_count):
    sample_index = lax.broadcasted_iota(jnp.int32, (length, bin_count), 0)
    bin_index = lax.broadcasted_iota(jnp.int32, (length, bin_count), 1) + first_bin
    phase_step = sample_index * bin_index % length
    angles = phase_step.astype(jnp.float32) * (2.0 * math.pi / length)
    return jnp.concatenate([jnp.cos(angles), -jnp.sin(angles)], axis=1).astype(jnp.bfloat16)


def finish(spectrum, band_low, band_high, channels, windows):
    bin_total = spectrum.shape[1]
    magnitude = jnp.sqrt(spectrum[0] * spectrum[0] + spectrum[1] * spectrum[1])
    padded = jnp.pad(magnitude, ((SMOOTH, SMOOTH), (0, 0)))
    summed = padded[0:bin_total]
    for offset in range(1, 2 * SMOOTH + 1):
        summed = summed + padded[offset : offset + bin_total]
    bin_column = lax.broadcasted_iota(jnp.int32, (bin_total, 1), 0)
    in_range = (
        jnp.minimum(bin_column + SMOOTH, bin_total - 1) - jnp.maximum(bin_column - SMOOTH, 0) + 1
    )
    smoothed = summed / in_range.astype(jnp.float32)
    divisor = jnp.maximum(smoothed, 1.0).reshape(bin_total, channels, windows)
    bin_index = lax.broadcasted_iota(jnp.int32, (bin_total, channels, 1), 0)
    inside = (
        (bin_index >= band_low[None, :, None]) & (bin_index < band_high[None, :, None])
    ).astype(jnp.float32)
    shaped = spectrum.reshape(2, bin_total, channels, windows)
    return (
        (shaped / divisor * inside).astype(jnp.bfloat16).reshape(2, bin_total, channels * windows)
    )


def whiten(records, window_valid, band_low, band_high):
    channels, windows, length = records.shape
    bin_total = length // 2
    row_total = channels * windows
    one_bit = (jnp.sign(records.astype(jnp.float32)) * window_valid[:, :, None]).astype(
        jnp.bfloat16
    )
    one_bit = one_bit.reshape(row_total, length)
    blocks = []
    for first_bin in range(0, bin_total, 256):
        dft_block = dft_table(length, first_bin, 256)
        partial_spec = lax.dot_general(
            dft_block, one_bit, (((0,), (1,)), ((), ())), preferred_element_type=jnp.float32
        )
        blocks.append(partial_spec.reshape(2, 256, row_total))
    spectrum = jnp.concatenate(blocks, axis=1)
    return finish(spectrum, band_low, band_high, channels, windows)


def cross_stack(first_spec, second_spec, first_flags, second_flags, in_use):
    real_part = jnp.einsum(
        "fsim,fsjm->sfij", first_spec[0], second_spec[0], preferred_element_type=jnp.float32
    )
    real_part = real_part + jnp.einsum(
        "fsim,fsjm->sfij", first_spec[1], second_spec[1], preferred_element_type=jnp.float32
    )
    imag_part = jnp.einsum(
        "fsim,fsjm->sfij", first_spec[1], second_spec[0], preferred_element_type=jnp.float32
    )
    imag_part = imag_part - jnp.einsum(
        "fsim,fsjm->sfij", first_spec[0], second_spec[1], preferred_element_type=jnp.float32
    )
    common = jnp.einsum("sim,sjm->sij", first_flags, second_flags, precision=lax.Precision.HIGHEST)
    weight = in_use[:, None, None] / jnp.maximum(common, 1.0)
    both = jnp.stack([real_part, imag_part], axis=2) * weight[:, None, None]
    return both.reshape(both.shape[0], both.shape[1], -1).astype(jnp.bfloat16)


def body(records, window_valid, band_low, band_high, pair_counts, partners):
    channels, windows, length = records.shape
    bin_total = length // 2
    readers, slot_count = partners.shape
    bin_share = bin_total // readers
    whitened = whiten(records, window_valid, band_low, band_high)
    arrived = lax.all_to_all(whitened, "chan", split_axis=1, concat_axis=2, tiled=True)
    spectra = arrived.reshape(2, bin_share, readers, channels, windows)
    copies = jnp.broadcast_to(window_valid[None], (readers, channels, windows))
    valid_all = lax.all_to_all(copies, "chan", split_axis=0, concat_axis=0, tiled=True)
    results = []
    for slot_index in range(slot_count):
        partner_ids = partners[:, slot_index]
        picks = partner_ids[:, None] == jnp.arange(readers, dtype=jnp.int32)[None, :]
        partner_spec = jnp.einsum("rq,cfqim->cfrim", picks.astype(jnp.bfloat16), spectra)
        partner_flags = jnp.einsum(
            "rq,qim->rim", picks.astype(jnp.float32), valid_all, precision=lax.Precision.HIGHEST
        )
        in_use = (slot_index < pair_counts).astype(jnp.float32)
        results.append(cross_stack(spectra, partner_spec, valid_all, partner_flags, in_use))
    stacked = jnp.stack(results, axis=1)
    return lax.all_to_all(stacked, "chan", split_axis=0, concat_axis=2, tiled=True)


LANES = 128


def lane_bins(share):
    lane = np.arange(LANES) % share
    half = share // 2
    even_first = 2 * (lane % half) + (lane >= half)
    odd_first = 2 * (lane % half) + (lane < half)
    return even_first, odd_first


def packed_table(length, share, readers):
    half = share // 2
    samples = np.arange(length // 2)
    tables = []
    for quad in range(readers // 4):
        for odd in range(2):
            columns = []
            for chunk in (2 * quad, 2 * quad + 1):
                order = (2 * chunk + 1, 2 * chunk) if odd else (2 * chunk, 2 * chunk + 1)
                bins = np.concatenate([t * share + 2 * np.arange(half) + odd for t in order])
                phase = (samples[:, None] * bins[None, :]) % length
                angles = phase.astype(np.float32) * np.float32(2.0 * math.pi / length)
                columns += [np.cos(angles), -np.sin(angles)]
            tables.append(np.concatenate(columns, axis=1))
    return np.stack(tables).reshape(readers // 4, 2, length // 2, 2 * LANES).astype(ml_dtypes.bfloat16)


def packed_band(share):
    half = share // 2
    even = 2 * np.arange(half)
    inner = np.concatenate([even, share + even, share + even + 1, even + 1])
    rows = np.concatenate([inner - LANES, inner, inner + LANES])
    even_first, odd_first = lane_bins(share)
    columns = np.concatenate([even_first, share + odd_first])
    near = np.abs(rows[:, None] - columns[None, :]) <= SMOOTH
    return near.astype(ml_dtypes.bfloat16)


def packed_fold(share):
    folds = [np.arange(share)[:, None] == order[None, :] for order in lane_bins(share)]
    return np.stack([np.concatenate([fold, fold], axis=1) for fold in folds]).astype(
        ml_dtypes.bfloat16
    )


def packed_spread(channels):
    lane = np.arange(LANES) % (channels * channels)
    rows = np.arange(channels)[:, None]
    return np.stack([rows == lane // channels, rows == lane % channels]).astype(np.float32)


def fused_kernel(
    n,
    bin_total,
    records_in,
    valid_in,
    low_in,
    high_in,
    counts_in,
    partners_in,
    table,
    band_in,
    fold_in,
    spread_in,
    out,
    records,
    valid,
    low,
    high,
    counts,
    partners,
    band,
    fold,
    spread,
    tables,
    signs,
    spec,
    mags,
    moved,
    send,
    recv,
    valids,
    row_flags,
    column_flags,
    full,
    turned,
    compact,
    stacked,
    state,
    table_sem,
    valid_send,
    valid_recv,
    spec_send,
    spec_recv,
    out_send,
    out_recv,
    own_sem,
    in_sem,
):
    me = lax.axis_index("chan")
    channels, windows, length = records.shape
    share = bin_total // n
    rows = channels * windows
    slots = partners.shape[0]
    chunks = n // 2
    quads = n // 4
    samples = length // 2

    def far_near(count, step):
        return jnp.where(step % 2 == 0, count // 2 + step // 2, count // 2 - 1 - step // 2)

    def peer(step):
        return me ^ step

    barrier = pltpu.get_barrier_semaphore()
    for step in range(1, n):
        pl.semaphore_signal(
            barrier, inc=1, device_id={"chan": peer(step)}, device_id_type=pl.DeviceIdType.MESH
        )

    def table_copy(quad):
        return pltpu.make_async_copy(table.at[quad], tables.at[quad], table_sem.at[quad])

    inputs = [
        pltpu.make_async_copy(source, target, in_sem.at[i])
        for i, (source, target) in enumerate(
            [
                (valid_in, valid),
                (records_in, records),
                (low_in, low),
                (high_in, high),
                (counts_in, counts),
                (partners_in, partners),
                (band_in, band),
                (fold_in, fold),
                (spread_in, spread),
            ]
        )
    ]
    for copy in inputs:
        copy.start()
    for quad in range(quads):
        table_copy(quad).start()
    for copy in inputs:
        copy.wait()

    valids[me] = valid[...]

    row = lax.broadcasted_iota(jnp.int32, (rows, windows), 0)
    window_lane = lax.broadcasted_iota(jnp.int32, (rows, windows), 1)
    spread_valid = jnp.broadcast_to(valid[...][:, None, :], (channels, windows, windows))
    spread_valid = spread_valid.reshape(rows, windows)
    level = jnp.sum(
        jnp.where(row % windows == window_lane, spread_valid, 0.0), axis=1, keepdims=True
    )
    level = jnp.broadcast_to(level, (rows, LANES)).astype(jnp.bfloat16)

    def to_signs(part, _):
        at = pl.multiple_of(part * LANES, LANES)
        later = pl.multiple_of(samples + part * LANES, LANES)

        def sign(x):
            one = jnp.ones_like(x)
            return jnp.where(x > 0, one, jnp.where(x < 0, -one, jnp.zeros_like(x)))

        a = sign(records[:, :, pl.ds(at, LANES)].reshape(rows, LANES))
        b = sign(records[:, :, pl.ds(later, LANES)].reshape(rows, LANES))
        signs[0, :, pl.ds(at, LANES)] = (a + b) * level
        signs[1, :, pl.ds(at, LANES)] = (a - b) * level
        return 0

    lax.fori_loop(0, samples // LANES, to_signs, 0)

    lane = lax.broadcasted_iota(jnp.int32, (1, LANES), 1)
    first = lane < share
    inner = lane % share
    front = inner < share // 2

    mags[:, 0:LANES] = jnp.zeros((rows, LANES), jnp.bfloat16)
    mags[:, (chunks + 1) * LANES : (chunks + 2) * LANES] = jnp.zeros((rows, LANES), jnp.bfloat16)

    def transform(quad, _):
        table_copy(quad).wait()
        even = jnp.dot(signs[0], tables[quad, 0], preferred_element_type=jnp.float32)
        odd = jnp.dot(signs[1], tables[quad, 1], preferred_element_type=jnp.float32)
        for part in range(2):
            chunk = 2 * quad + part
            e = even[:, part * LANES : (part + 1) * LANES]
            o = odd[:, part * LANES : (part + 1) * LANES]
            spec[2 * chunk] = jnp.where(front, e, o)
            spec[2 * chunk + 1] = jnp.where(front, o, e)
            e, o = e * e, o * o
            e, o = e + pltpu.roll(e, share, 1), o + pltpu.roll(o, share, 1)
            at = pl.multiple_of((chunk + 1) * LANES, LANES)
            mags[:, pl.ds(at, LANES)] = jnp.sqrt(jnp.where(first, e, o)).astype(jnp.bfloat16)
        return 0

    lax.fori_loop(0, quads, transform, 0)

    pl.semaphore_wait(barrier, n - 1)

    def valid_copy(source, target):
        return pltpu.make_async_remote_copy(
            src_ref=valids.at[source],
            dst_ref=valids.at[source],
            send_sem=valid_send.at[target],
            recv_sem=valid_recv.at[source],
            device_id={"chan": target},
            device_id_type=pl.DeviceIdType.MESH,
        )

    def spec_copy(source, target):
        return pltpu.make_async_remote_copy(
            src_ref=send.at[target],
            dst_ref=recv.at[source],
            send_sem=spec_send.at[target],
            recv_sem=spec_recv.at[source],
            device_id={"chan": target},
            device_id_type=pl.DeviceIdType.MESH,
        )

    def out_copy(source, target):
        at = pl.multiple_of(source * share, share)
        return pltpu.make_async_remote_copy(
            src_ref=stacked.at[target],
            dst_ref=out.at[:, pl.ds(at, share), :],
            send_sem=out_send.at[target],
            recv_sem=out_recv.at[source],
            device_id={"chan": target},
            device_id_type=pl.DeviceIdType.MESH,
        )

    channel = lax.broadcasted_iota(jnp.int32, (channels, 1), 0)
    lows = jnp.zeros((channels, 1), jnp.int32)
    highs = jnp.zeros((channels, 1), jnp.int32)
    for c in range(channels):
        lows = jnp.where(channel == c, low[c], lows)
        highs = jnp.where(channel == c, high[c], highs)

    def whiten(chunk):
        at = pl.multiple_of(chunk * LANES, LANES)
        total = jnp.dot(
            mags[:, pl.ds(at, 3 * LANES)], band[...], preferred_element_type=jnp.float32
        )
        for part in range(2):
            target = 2 * chunk + part
            k = target * share + 2 * (inner % (share // 2))
            k = k + jnp.where(front, part, 1 - part)
            near = jnp.minimum(k + SMOOTH, bin_total - 1) - jnp.maximum(k - SMOOTH, 0) + 1
            smoothed = total[:, part * LANES : (part + 1) * LANES] * (1.0 / near.astype(jnp.float32))
            inside = jnp.where((k >= lows) & (k < highs), 1.0, 0.0)
            y = spec[target] / jnp.maximum(smoothed, 1.0)
            y = y.reshape(channels, windows, LANES) * inside[:, None, :]
            moved[part] = y.reshape(rows, LANES)
            for pair in range(windows // 2):
                both = [
                    moved[part, pl.ds(w, channels, stride=windows), :]
                    for w in (2 * pair, 2 * pair + 1)
                ]
                send[target, pl.ds(pair * 2 * channels, 2 * channels), :] = jnp.concatenate(
                    both, axis=0
                ).astype(jnp.bfloat16)

    def send_valid(step, _):
        valid_copy(me, peer(step)).start()
        return 0

    lax.fori_loop(1, n, send_valid, 0)

    def send_spec(step, _):
        chunk = (me // 2) ^ far_near(chunks, step)
        whiten(chunk)
        for part in range(2):
            target = 2 * chunk + part

            @pl.when(target != me)
            def _():
                spec_copy(me, target).start()

        return 0

    lax.fori_loop(0, chunks, send_spec, 0)

    def place(source, block):
        block = block.astype(jnp.float32)
        full[source] = block
        swapped = pltpu.roll(block, share, 1)
        turned[source] = jnp.where(first, -swapped, swapped)

    def spread_flags(source):
        flags = valids[source]
        for which, target in ((0, row_flags), (1, column_flags)):
            target[source] = lax.dot_general(
                flags,
                spread[which],
                (((0,), (0,)), ((), ())),
                precision=lax.Precision.HIGHEST,
                preferred_element_type=jnp.float32,
            )

    place(me, send[me])
    spread_flags(me)

    def receive_valid(step, _):
        source = peer(step)
        valid_copy(source, me).wait_recv()
        spread_flags(source)
        return 0

    lax.fori_loop(1, n, receive_valid, 0)

    def receive(step, _):
        source = me ^ far_near(n, step)
        spec_copy(source, me).wait_recv()
        place(source, recv[source])
        return 0

    lax.fori_loop(0, n - 1, receive, 0)

    folding = fold[me % 2]

    def order(place_index):
        return me ^ far_near(n, place_index)

    def stack_entry(entry):
        place_index = state[0]
        slot = state[1]
        reader = order(place_index % n)
        partner = partners[slot, reader]

        def window_step(window, totals):
            at = pl.multiple_of(window * channels, channels)
            straight = full[partner, pl.ds(at, channels), :]
            crossed = turned[partner, pl.ds(at, channels), :]
            totals = list(totals)
            for i in range(channels):
                own = full[reader, pl.ds(at + i, 1), :]
                totals[i] += own * straight
                totals[channels + i] += own * crossed
            return tuple(totals)

        zero = jnp.zeros((channels, LANES), jnp.float32)
        totals = lax.fori_loop(0, windows, window_step, (zero,) * (2 * channels), unroll=4)
        tile = jnp.concatenate(totals, axis=0)
        high_part = tile.astype(jnp.bfloat16)
        low_part = (tile - high_part.astype(jnp.float32)).astype(jnp.bfloat16)
        flat = lax.dot_general(
            folding,
            jnp.concatenate([high_part, low_part], axis=1),
            (((1,), (1,)), ((), ())),
            preferred_element_type=jnp.float32,
        )
        common = jnp.sum(row_flags[reader] * column_flags[partner], axis=0, keepdims=True)
        compact[entry] = (flat * (1.0 / jnp.maximum(common, 1.0))).astype(jnp.bfloat16)
        more = slot + 1 < counts[reader]
        state[0] = jnp.where(more, place_index, place_index + 1)
        state[1] = jnp.where(more, slot + 1, 0)

    entries = 2 * n
    ready = [min(slots * (p + 1), entries - (n - 1 - p)) for p in range(n)]
    added = [now - before for now, before in zip(ready, [0] + ready)]

    def send_stack(begin, shift, width, place_index, _):
        for extra in range(width):
            stack_entry(begin + (place_index - shift) * width + extra)
        base = state[2]
        reader = order(place_index)
        count = counts[reader]
        for slot in range(slots):
            block = compact[jnp.minimum(base + slot, entries - 1)]
            stacked[reader, slot] = jnp.where(slot < count, block, jnp.zeros_like(block))

        @pl.when(place_index < n - 1)
        def _():
            out_copy(me, reader).start()

        state[2] = base + count
        return 0

    for i in range(3):
        state[i] = 0
    p = 0
    while p < n:
        stop = p
        while stop < n and added[stop] == added[p]:
            stop += 1
        step = functools.partial(send_stack, ready[p] - added[p], p, added[p])
        lax.fori_loop(p, stop, step, 0)
        p = stop
    own_at = pl.multiple_of(me * share, share)
    own = pltpu.make_async_copy(stacked.at[me], out.at[:, pl.ds(own_at, share), :], own_sem)
    own.start()
    own.wait()

    def finish_copies(step, _):
        target = peer(step)
        valid_copy(me, target).wait_send()
        spec_copy(me, target).wait_send()
        out_copy(me, target).wait_send()
        out_copy(target, me).wait_recv()
        return 0

    lax.fori_loop(1, n, finish_copies, 0)


def fused(n, records, window_valid, band_low, band_high, pair_counts, partners):
    channels, windows, length = records.shape
    bin_total = length // 2
    slots = partners.shape[1]
    share = bin_total // n
    rows = channels * windows
    table = jnp.asarray(packed_table(length, share, n))
    band = jnp.asarray(packed_band(share))
    fold = jnp.asarray(packed_fold(share))
    spread = jnp.asarray(packed_spread(channels))
    hbm = pl.BlockSpec(memory_space=pltpu.HBM)
    dma = pltpu.SemaphoreType.DMA
    by_slot = partners.T
    out = pl.pallas_call(
        functools.partial(fused_kernel, n, bin_total),
        out_shape=jax.ShapeDtypeStruct((slots, bin_total, LANES), jnp.bfloat16),
        in_specs=[hbm] * 10,
        out_specs=pl.BlockSpec(memory_space=pl.ANY),
        scratch_shapes=[
            pltpu.VMEM(records.shape, jnp.bfloat16),
            pltpu.VMEM(window_valid.shape, jnp.float32),
            pltpu.SMEM(band_low.shape, jnp.int32),
            pltpu.SMEM(band_high.shape, jnp.int32),
            pltpu.SMEM(pair_counts.shape, jnp.int32),
            pltpu.SMEM(by_slot.shape, jnp.int32),
            pltpu.VMEM(band.shape, jnp.bfloat16),
            pltpu.VMEM(fold.shape, jnp.bfloat16),
            pltpu.VMEM(spread.shape, jnp.float32),
            pltpu.VMEM(table.shape, jnp.bfloat16),
            pltpu.VMEM((2, rows, length // 2), jnp.bfloat16),
            pltpu.VMEM((n, rows, LANES), jnp.float32),
            pltpu.VMEM((rows, (n // 2 + 2) * LANES), jnp.bfloat16),
            pltpu.VMEM((2, rows, LANES), jnp.float32),
            pltpu.VMEM((n, rows, LANES), jnp.bfloat16),
            pltpu.VMEM((n, rows, LANES), jnp.bfloat16),
            pltpu.VMEM((n, channels, windows), jnp.float32),
            pltpu.VMEM((n, windows, LANES), jnp.float32),
            pltpu.VMEM((n, windows, LANES), jnp.float32),
            pltpu.VMEM((n, rows, LANES), jnp.float32),
            pltpu.VMEM((n, rows, LANES), jnp.float32),
            pltpu.VMEM((2 * n, share, LANES), jnp.bfloat16),
            pltpu.VMEM((n, slots, share, LANES), jnp.bfloat16),
            pltpu.SMEM((3,), jnp.int32),
            dma((n // 4,)),
            dma((n,)),
            dma((n,)),
            dma((n,)),
            dma((n,)),
            dma((n,)),
            dma((n,)),
            dma,
            dma((9,)),
        ],
        compiler_params=pltpu.CompilerParams(
            collective_id=0, has_side_effects=True, vmem_limit_bytes=64 * 1024 * 1024
        ),
    )(records, window_valid, band_low, band_high, pair_counts, by_slot, table, band, fold, spread)
    return out[None]


def solution(mesh):
    def run(records, window_valid, band_low, band_high, pair_counts, partners):
        n = mesh.shape["chan"]
        channels, windows, length = records.shape
        whole_tiles = 2 * (length // 2 // n) == LANES and 2 * channels * channels == LANES
        args = (records, window_valid, band_low, band_high, pair_counts, partners)
        if whole_tiles and n >= 8 and n & (n - 1) == 0 and windows % 2 == 0:
            return fused(n, *args)
        return body(*args)

    return jax.shard_map(
        run,
        mesh=mesh,
        in_specs=(
            P(("groups", "chan"), None, None),
            P(("groups", "chan"), None),
            P(("groups", "chan")),
            P(("groups", "chan")),
            P("groups"),
            P("groups", None),
        ),
        out_specs=P(("groups", "chan"), None, None, None),
        check_vma=False,
    )
```

```python
import functools
import math

import jax
import jax.numpy as jnp
import ml_dtypes
import numpy as np
from jax import lax
from jax.experimental import pallas as pl
from jax.experimental.pallas import tpu as pltpu
from jax.sharding import PartitionSpec as P

SMOOTH = 8


def dft_table(length, first_bin, bin_count):
    sample_index = lax.broadcasted_iota(jnp.int32, (length, bin_count), 0)
    bin_index = lax.broadcasted_iota(jnp.int32, (length, bin_count), 1) + first_bin
    phase_step = sample_index * bin_index % length
    angles = phase_step.astype(jnp.float32) * (2.0 * math.pi / length)
    return jnp.concatenate([jnp.cos(angles), -jnp.sin(angles)], axis=1).astype(jnp.bfloat16)


def finish(spectrum, band_low, band_high, channels, windows):
    bin_total = spectrum.shape[1]
    magnitude = jnp.sqrt(spectrum[0] * spectrum[0] + spectrum[1] * spectrum[1])
    padded = jnp.pad(magnitude, ((SMOOTH, SMOOTH), (0, 0)))
    summed = padded[0:bin_total]
    for offset in range(1, 2 * SMOOTH + 1):
        summed = summed + padded[offset : offset + bin_total]
    bin_column = lax.broadcasted_iota(jnp.int32, (bin_total, 1), 0)
    in_range = (
        jnp.minimum(bin_column + SMOOTH, bin_total - 1) - jnp.maximum(bin_column - SMOOTH, 0) + 1
    )
    smoothed = summed / in_range.astype(jnp.float32)
    divisor = jnp.maximum(smoothed, 1.0).reshape(bin_total, channels, windows)
    bin_index = lax.broadcasted_iota(jnp.int32, (bin_total, channels, 1), 0)
    inside = (
        (bin_index >= band_low[None, :, None]) & (bin_index < band_high[None, :, None])
    ).astype(jnp.float32)
    shaped = spectrum.reshape(2, bin_total, channels, windows)
    return (
        (shaped / divisor * inside).astype(jnp.bfloat16).reshape(2, bin_total, channels * windows)
    )


def whiten(records, window_valid, band_low, band_high):
    channels, windows, length = records.shape
    bin_total = length // 2
    row_total = channels * windows
    one_bit = (jnp.sign(records.astype(jnp.float32)) * window_valid[:, :, None]).astype(
        jnp.bfloat16
    )
    one_bit = one_bit.reshape(row_total, length)
    blocks = []
    for first_bin in range(0, bin_total, 256):
        dft_block = dft_table(length, first_bin, 256)
        partial_spec = lax.dot_general(
            dft_block, one_bit, (((0,), (1,)), ((), ())), preferred_element_type=jnp.float32
        )
        blocks.append(partial_spec.reshape(2, 256, row_total))
    spectrum = jnp.concatenate(blocks, axis=1)
    return finish(spectrum, band_low, band_high, channels, windows)


def cross_stack(first_spec, second_spec, first_flags, second_flags, in_use):
    real_part = jnp.einsum(
        "fsim,fsjm->sfij", first_spec[0], second_spec[0], preferred_element_type=jnp.float32
    )
    real_part = real_part + jnp.einsum(
        "fsim,fsjm->sfij", first_spec[1], second_spec[1], preferred_element_type=jnp.float32
    )
    imag_part = jnp.einsum(
        "fsim,fsjm->sfij", first_spec[1], second_spec[0], preferred_element_type=jnp.float32
    )
    imag_part = imag_part - jnp.einsum(
        "fsim,fsjm->sfij", first_spec[0], second_spec[1], preferred_element_type=jnp.float32
    )
    common = jnp.einsum("sim,sjm->sij", first_flags, second_flags, precision=lax.Precision.HIGHEST)
    weight = in_use[:, None, None] / jnp.maximum(common, 1.0)
    both = jnp.stack([real_part, imag_part], axis=2) * weight[:, None, None]
    return both.reshape(both.shape[0], both.shape[1], -1).astype(jnp.bfloat16)


def body(records, window_valid, band_low, band_high, pair_counts, partners):
    channels, windows, length = records.shape
    bin_total = length // 2
    readers, slot_count = partners.shape
    bin_share = bin_total // readers
    whitened = whiten(records, window_valid, band_low, band_high)
    arrived = lax.all_to_all(whitened, "chan", split_axis=1, concat_axis=2, tiled=True)
    spectra = arrived.reshape(2, bin_share, readers, channels, windows)
    copies = jnp.broadcast_to(window_valid[None], (readers, channels, windows))
    valid_all = lax.all_to_all(copies, "chan", split_axis=0, concat_axis=0, tiled=True)
    results = []
    for slot_index in range(slot_count):
        partner_ids = partners[:, slot_index]
        picks = partner_ids[:, None] == jnp.arange(readers, dtype=jnp.int32)[None, :]
        partner_spec = jnp.einsum("rq,cfqim->cfrim", picks.astype(jnp.bfloat16), spectra)
        partner_flags = jnp.einsum(
            "rq,qim->rim", picks.astype(jnp.float32), valid_all, precision=lax.Precision.HIGHEST
        )
        in_use = (slot_index < pair_counts).astype(jnp.float32)
        results.append(cross_stack(spectra, partner_spec, valid_all, partner_flags, in_use))
    stacked = jnp.stack(results, axis=1)
    return lax.all_to_all(stacked, "chan", split_axis=0, concat_axis=2, tiled=True)


LANES = 128


def lane_bins(share):
    lane = np.arange(LANES) % share
    half = share // 2
    even_first = 2 * (lane % half) + (lane >= half)
    odd_first = 2 * (lane % half) + (lane < half)
    return even_first, odd_first


def packed_table(length, share, readers):
    half = share // 2
    samples = np.arange(length // 2)
    tables = []
    for quad in range(readers // 4):
        for odd in range(2):
            columns = []
            for chunk in (2 * quad, 2 * quad + 1):
                order = (2 * chunk + 1, 2 * chunk) if odd else (2 * chunk, 2 * chunk + 1)
                bins = np.concatenate([t * share + 2 * np.arange(half) + odd for t in order])
                phase = (samples[:, None] * bins[None, :]) % length
                angles = phase.astype(np.float32) * np.float32(2.0 * math.pi / length)
                columns += [np.cos(angles), -np.sin(angles)]
            tables.append(np.concatenate(columns, axis=1))
    return np.stack(tables).reshape(readers // 4, 2, length // 2, 2 * LANES).astype(ml_dtypes.bfloat16)


def packed_band(share):
    half = share // 2
    even = 2 * np.arange(half)
    inner = np.concatenate([even, share + even, share + even + 1, even + 1])
    rows = np.concatenate([inner - LANES, inner, inner + LANES])
    even_first, odd_first = lane_bins(share)
    columns = np.concatenate([even_first, share + odd_first])
    near = np.abs(rows[:, None] - columns[None, :]) <= SMOOTH
    return near.astype(ml_dtypes.bfloat16)


def packed_fold(share):
    folds = [np.arange(share)[:, None] == order[None, :] for order in lane_bins(share)]
    return np.stack([np.concatenate([fold, fold], axis=1) for fold in folds]).astype(
        ml_dtypes.bfloat16
    )


def packed_spread(channels):
    lane = np.arange(LANES) % (channels * channels)
    rows = np.arange(channels)[:, None]
    both = np.concatenate([rows == lane // channels, rows == lane % channels], axis=1)
    return np.concatenate([both] * 3).astype(ml_dtypes.bfloat16)


def fused_kernel(
    n,
    bin_total,
    records_in,
    valid_in,
    low_in,
    high_in,
    counts_in,
    partners_in,
    table,
    band_in,
    fold_in,
    spread_in,
    out,
    records,
    valid,
    low,
    high,
    counts,
    partners,
    band,
    fold,
    spread,
    tables,
    signs,
    spec,
    mags,
    moved,
    send,
    recv,
    valids,
    flags,
    full,
    turned,
    compact,
    stacked,
    state,
    table_sem,
    valid_send,
    valid_recv,
    spec_send,
    spec_recv,
    out_send,
    out_recv,
    in_sem,
):
    me = lax.axis_index("chan")
    channels, windows, length = records.shape
    share = bin_total // n
    rows = channels * windows
    slots = partners.shape[0]
    chunks = n // 2
    quads = n // 4
    samples = length // 2

    def far_near(count, step):
        return jnp.where(step % 2 == 0, count // 2 + step // 2, count // 2 - 1 - step // 2)

    def peer(step):
        return me ^ step

    barrier = pltpu.get_barrier_semaphore()
    for step in range(1, n):
        pl.semaphore_signal(
            barrier, inc=1, device_id={"chan": peer(step)}, device_id_type=pl.DeviceIdType.MESH
        )

    def table_copy(quad):
        return pltpu.make_async_copy(table.at[quad], tables.at[quad], table_sem.at[quad])

    inputs = [
        pltpu.make_async_copy(source, target, in_sem.at[i])
        for i, (source, target) in enumerate(
            [
                (valid_in, valid),
                (records_in, records),
                (low_in, low),
                (high_in, high),
                (counts_in, counts),
                (partners_in, partners),
                (band_in, band),
                (fold_in, fold),
                (spread_in, spread),
            ]
        )
    ]
    for copy in inputs:
        copy.start()
    for quad in range(quads):
        table_copy(quad).start()
    for copy in inputs:
        copy.wait()

    valids[me] = valid[...]

    row = lax.broadcasted_iota(jnp.int32, (rows, windows), 0)
    window_lane = lax.broadcasted_iota(jnp.int32, (rows, windows), 1)
    spread_valid = jnp.broadcast_to(valid[...][:, None, :], (channels, windows, windows))
    spread_valid = spread_valid.reshape(rows, windows)
    level = jnp.sum(
        jnp.where(row % windows == window_lane, spread_valid, 0.0), axis=1, keepdims=True
    )
    level = jnp.broadcast_to(level, (rows, LANES)).astype(jnp.bfloat16)

    def to_signs(part, _):
        at = pl.multiple_of(part * LANES, LANES)
        later = pl.multiple_of(samples + part * LANES, LANES)

        def sign(x):
            one = jnp.ones_like(x)
            return jnp.where(x > 0, one, jnp.where(x < 0, -one, jnp.zeros_like(x)))

        a = sign(records[:, :, pl.ds(at, LANES)].reshape(rows, LANES))
        b = sign(records[:, :, pl.ds(later, LANES)].reshape(rows, LANES))
        signs[0, :, pl.ds(at, LANES)] = (a + b) * level
        signs[1, :, pl.ds(at, LANES)] = (a - b) * level
        return 0

    lax.fori_loop(0, samples // LANES, to_signs, 0)

    lane = lax.broadcasted_iota(jnp.int32, (1, LANES), 1)
    first = lane < share
    inner = lane % share
    front = inner < share // 2

    mags[:, 0:LANES] = jnp.zeros((rows, LANES), jnp.bfloat16)
    mags[:, (chunks + 1) * LANES : (chunks + 2) * LANES] = jnp.zeros((rows, LANES), jnp.bfloat16)

    def transform(quad, _):
        table_copy(quad).wait()
        even = jnp.dot(signs[0], tables[quad, 0], preferred_element_type=jnp.float32)
        odd = jnp.dot(signs[1], tables[quad, 1], preferred_element_type=jnp.float32)
        for part in range(2):
            chunk = 2 * quad + part
            e = even[:, part * LANES : (part + 1) * LANES]
            o = odd[:, part * LANES : (part + 1) * LANES]
            spec[2 * chunk] = jnp.where(front, e, o)
            spec[2 * chunk + 1] = jnp.where(front, o, e)
            e, o = e * e, o * o
            e, o = e + pltpu.roll(e, share, 1), o + pltpu.roll(o, share, 1)
            at = pl.multiple_of((chunk + 1) * LANES, LANES)
            mags[:, pl.ds(at, LANES)] = jnp.sqrt(jnp.where(first, e, o)).astype(jnp.bfloat16)
        return 0

    lax.fori_loop(0, quads, transform, 0)

    pl.semaphore_wait(barrier, n - 1)

    def valid_copy(source, target):
        return pltpu.make_async_remote_copy(
            src_ref=valids.at[source],
            dst_ref=valids.at[source],
            send_sem=valid_send.at[target],
            recv_sem=valid_recv.at[source],
            device_id={"chan": target},
            device_id_type=pl.DeviceIdType.MESH,
        )

    def spec_copy(source, target):
        return pltpu.make_async_remote_copy(
            src_ref=send.at[target],
            dst_ref=recv.at[source],
            send_sem=spec_send.at[target],
            recv_sem=spec_recv.at[source],
            device_id={"chan": target},
            device_id_type=pl.DeviceIdType.MESH,
        )

    def out_copy(source, target):
        at = pl.multiple_of(source * share, share)
        return pltpu.make_async_remote_copy(
            src_ref=stacked.at[target],
            dst_ref=out.at[:, pl.ds(at, share), :],
            send_sem=out_send.at[target],
            recv_sem=out_recv.at[source],
            device_id={"chan": target},
            device_id_type=pl.DeviceIdType.MESH,
        )

    channel = lax.broadcasted_iota(jnp.int32, (channels, 1), 0)
    lows = jnp.zeros((channels, 1), jnp.int32)
    highs = jnp.zeros((channels, 1), jnp.int32)
    for c in range(channels):
        lows = jnp.where(channel == c, low[c], lows)
        highs = jnp.where(channel == c, high[c], highs)

    def whiten(chunk):
        at = pl.multiple_of(chunk * LANES, LANES)
        total = jnp.dot(
            mags[:, pl.ds(at, 3 * LANES)], band[...], preferred_element_type=jnp.float32
        )
        for part in range(2):
            target = 2 * chunk + part
            k = target * share + 2 * (inner % (share // 2))
            k = k + jnp.where(front, part, 1 - part)
            near = jnp.minimum(k + SMOOTH, bin_total - 1) - jnp.maximum(k - SMOOTH, 0) + 1
            smoothed = total[:, part * LANES : (part + 1) * LANES] * (1.0 / near.astype(jnp.float32))
            inside = jnp.where((k >= lows) & (k < highs), 1.0, 0.0)
            y = spec[target] / jnp.maximum(smoothed, 1.0)
            y = y.reshape(channels, windows, LANES) * inside[:, None, :]
            send[target] = y.reshape(rows, LANES).astype(jnp.bfloat16)

    def send_spec(step, _):
        chunk = (me // 2) ^ far_near(chunks, step)
        whiten(chunk)
        for part in range(2):
            target = 2 * chunk + part

            @pl.when(target != me)
            def _():
                spec_copy(me, target).start()
                valid_copy(me, target).start()

        return 0

    lax.fori_loop(0, chunks, send_spec, 0)

    def place(source, block):
        moved[...] = block.astype(jnp.float32)
        for window in range(windows):
            part = moved[pl.ds(window, channels, stride=windows), :]
            swapped = pltpu.roll(part, share, 1)
            full[source, window * channels : (window + 1) * channels] = part
            turned[source, window * channels : (window + 1) * channels] = jnp.where(
                first, -swapped, swapped
            )
        pieces = []
        rest = valids[source]
        for _ in range(3):
            piece = rest.astype(jnp.bfloat16)
            rest = rest - piece.astype(jnp.float32)
            pieces.append(piece)
        flags[source] = lax.dot_general(
            jnp.concatenate(pieces, axis=0),
            spread[...],
            (((0,), (0,)), ((), ())),
            preferred_element_type=jnp.float32,
        )

    place(me, send[me])

    def receive(step, _):
        source = me ^ far_near(n, step)
        spec_copy(source, me).wait_recv()
        valid_copy(source, me).wait_recv()
        place(source, recv[source])
        return 0

    lax.fori_loop(0, n - 1, receive, 0)

    folding = fold[me % 2]

    def order(place_index):
        return me ^ far_near(n, place_index)

    def stack_entry(entry):
        place_index = state[0]
        slot = state[1]
        reader = order(place_index % n)
        partner = partners[slot, reader]

        def window_step(window, totals):
            at = pl.multiple_of(window * channels, channels)
            straight = full[partner, pl.ds(at, channels), :]
            crossed = turned[partner, pl.ds(at, channels), :]
            totals = list(totals)
            for i in range(channels):
                own = full[reader, pl.ds(at + i, 1), :]
                totals[i] += own * straight
                totals[channels + i] += own * crossed
            return tuple(totals)

        zero = jnp.zeros((channels, LANES), jnp.float32)
        totals = lax.fori_loop(0, windows, window_step, (zero,) * (2 * channels), unroll=4)
        tile = jnp.concatenate(totals, axis=0)
        high_part = tile.astype(jnp.bfloat16)
        low_part = (tile - high_part.astype(jnp.float32)).astype(jnp.bfloat16)
        flat = lax.dot_general(
            folding,
            jnp.concatenate([high_part, low_part], axis=1),
            (((1,), (1,)), ((), ())),
            preferred_element_type=jnp.float32,
        )
        common = flags[reader, :, 0:LANES] * flags[partner, :, LANES : 2 * LANES]
        common = jnp.sum(common, axis=0, keepdims=True)
        compact[entry] = (flat * (1.0 / jnp.maximum(common, 1.0))).astype(jnp.bfloat16)
        more = slot + 1 < counts[reader]
        state[0] = jnp.where(more, place_index, place_index + 1)
        state[1] = jnp.where(more, slot + 1, 0)

    entries = 2 * n
    ready = [min(slots * (p + 1), entries - (n - 1 - p)) for p in range(n)]
    added = [now - before for now, before in zip(ready, [0] + ready)]

    def send_stack(begin, shift, width, place_index, _):
        for extra in range(width):
            stack_entry(begin + (place_index - shift) * width + extra)
        base = state[2]
        reader = order(place_index)
        count = counts[reader]
        for slot in range(slots):
            block = compact[jnp.minimum(base + slot, entries - 1)]
            stacked[reader, slot] = jnp.where(slot < count, block, jnp.zeros_like(block))

        @pl.when(place_index < n - 1)
        def _():
            out_copy(me, reader).start()

        state[2] = base + count
        return 0

    for i in range(3):
        state[i] = 0
    p = 0
    while p < n:
        stop = p
        while stop < n and added[stop] == added[p]:
            stop += 1
        step = functools.partial(send_stack, ready[p] - added[p], p, added[p])
        lax.fori_loop(p, stop, step, 0)
        p = stop
    own_at = pl.multiple_of(me * share, share)
    out[:, pl.ds(own_at, share), :] = stacked[me]

    def finish_copies(step, _):
        target = peer(step)
        valid_copy(me, target).wait_send()
        spec_copy(me, target).wait_send()
        out_copy(me, target).wait_send()
        out_copy(target, me).wait_recv()
        return 0

    lax.fori_loop(1, n, finish_copies, 0)


def fused(n, records, window_valid, band_low, band_high, pair_counts, partners):
    channels, windows, length = records.shape
    bin_total = length // 2
    slots = partners.shape[1]
    share = bin_total // n
    rows = channels * windows
    table = jnp.asarray(packed_table(length, share, n))
    band = jnp.asarray(packed_band(share))
    fold = jnp.asarray(packed_fold(share))
    spread = jnp.asarray(packed_spread(channels))
    hbm = pl.BlockSpec(memory_space=pltpu.HBM)
    dma = pltpu.SemaphoreType.DMA
    by_slot = partners.T
    out = pl.pallas_call(
        functools.partial(fused_kernel, n, bin_total),
        out_shape=pltpu.VMEM((slots, bin_total, LANES), jnp.bfloat16),
        in_specs=[hbm] * 10,
        out_specs=pl.BlockSpec(memory_space=pltpu.VMEM),
        scratch_shapes=[
            pltpu.VMEM(records.shape, jnp.bfloat16),
            pltpu.VMEM(window_valid.shape, jnp.float32),
            pltpu.SMEM(band_low.shape, jnp.int32),
            pltpu.SMEM(band_high.shape, jnp.int32),
            pltpu.SMEM(pair_counts.shape, jnp.int32),
            pltpu.SMEM(by_slot.shape, jnp.int32),
            pltpu.VMEM(band.shape, jnp.bfloat16),
            pltpu.VMEM(fold.shape, jnp.bfloat16),
            pltpu.VMEM(spread.shape, jnp.bfloat16),
            pltpu.VMEM(table.shape, jnp.bfloat16),
            pltpu.VMEM((2, rows, length // 2), jnp.bfloat16),
            pltpu.VMEM((n, rows, LANES), jnp.float32),
            pltpu.VMEM((rows, (n // 2 + 2) * LANES), jnp.bfloat16),
            pltpu.VMEM((rows, LANES), jnp.float32),
            pltpu.VMEM((n, rows, LANES), jnp.bfloat16),
            pltpu.VMEM((n, rows, LANES), jnp.bfloat16),
            pltpu.VMEM((n, channels, windows), jnp.float32),
            pltpu.VMEM((n, windows, 2 * LANES), jnp.float32),
            pltpu.VMEM((n, rows, LANES), jnp.float32),
            pltpu.VMEM((n, rows, LANES), jnp.float32),
            pltpu.VMEM((2 * n, share, LANES), jnp.bfloat16),
            pltpu.VMEM((n, slots, share, LANES), jnp.bfloat16),
            pltpu.SMEM((3,), jnp.int32),
            dma((n // 4,)),
            dma((n,)),
            dma((n,)),
            dma((n,)),
            dma((n,)),
            dma((n,)),
            dma((n,)),
            dma((9,)),
        ],
        compiler_params=pltpu.CompilerParams(
            collective_id=0, has_side_effects=True, vmem_limit_bytes=60 * 1024 * 1024
        ),
    )(records, window_valid, band_low, band_high, pair_counts, by_slot, table, band, fold, spread)
    return out[None]


def solution(mesh):
    def run(records, window_valid, band_low, band_high, pair_counts, partners):
        n = mesh.shape["chan"]
        channels, windows, length = records.shape
        whole_tiles = 2 * (length // 2 // n) == LANES and 2 * channels * channels == LANES
        args = (records, window_valid, band_low, band_high, pair_counts, partners)
        if whole_tiles and n >= 8 and n & (n - 1) == 0 and windows % 2 == 0:
            return fused(n, *args)
        return body(*args)

    return jax.shard_map(
        run,
        mesh=mesh,
        in_specs=(
            P(("groups", "chan"), None, None),
            P(("groups", "chan"), None),
            P(("groups", "chan")),
            P(("groups", "chan")),
            P("groups"),
            P("groups", None),
        ),
        out_specs=P(("groups", "chan"), None, None, None),
        check_vma=False,
    )
```

```python
import functools
import math

import jax
import jax.numpy as jnp
import ml_dtypes
import numpy as np
from jax import lax
from jax.experimental import pallas as pl
from jax.experimental.pallas import tpu as pltpu
from jax.sharding import PartitionSpec as P

SMOOTH = 8


def dft_table(length, first_bin, bin_count):
    sample_index = lax.broadcasted_iota(jnp.int32, (length, bin_count), 0)
    bin_index = lax.broadcasted_iota(jnp.int32, (length, bin_count), 1) + first_bin
    phase_step = sample_index * bin_index % length
    angles = phase_step.astype(jnp.float32) * (2.0 * math.pi / length)
    return jnp.concatenate([jnp.cos(angles), -jnp.sin(angles)], axis=1).astype(jnp.bfloat16)


def finish(spectrum, band_low, band_high, channels, windows):
    bin_total = spectrum.shape[1]
    magnitude = jnp.sqrt(spectrum[0] * spectrum[0] + spectrum[1] * spectrum[1])
    padded = jnp.pad(magnitude, ((SMOOTH, SMOOTH), (0, 0)))
    summed = padded[0:bin_total]
    for offset in range(1, 2 * SMOOTH + 1):
        summed = summed + padded[offset : offset + bin_total]
    bin_column = lax.broadcasted_iota(jnp.int32, (bin_total, 1), 0)
    in_range = (
        jnp.minimum(bin_column + SMOOTH, bin_total - 1) - jnp.maximum(bin_column - SMOOTH, 0) + 1
    )
    smoothed = summed / in_range.astype(jnp.float32)
    divisor = jnp.maximum(smoothed, 1.0).reshape(bin_total, channels, windows)
    bin_index = lax.broadcasted_iota(jnp.int32, (bin_total, channels, 1), 0)
    inside = (
        (bin_index >= band_low[None, :, None]) & (bin_index < band_high[None, :, None])
    ).astype(jnp.float32)
    shaped = spectrum.reshape(2, bin_total, channels, windows)
    return (
        (shaped / divisor * inside).astype(jnp.bfloat16).reshape(2, bin_total, channels * windows)
    )


def whiten(records, window_valid, band_low, band_high):
    channels, windows, length = records.shape
    bin_total = length // 2
    row_total = channels * windows
    one_bit = (jnp.sign(records.astype(jnp.float32)) * window_valid[:, :, None]).astype(
        jnp.bfloat16
    )
    one_bit = one_bit.reshape(row_total, length)
    blocks = []
    for first_bin in range(0, bin_total, 256):
        dft_block = dft_table(length, first_bin, 256)
        partial_spec = lax.dot_general(
            dft_block, one_bit, (((0,), (1,)), ((), ())), preferred_element_type=jnp.float32
        )
        blocks.append(partial_spec.reshape(2, 256, row_total))
    spectrum = jnp.concatenate(blocks, axis=1)
    return finish(spectrum, band_low, band_high, channels, windows)


def cross_stack(first_spec, second_spec, first_flags, second_flags, in_use):
    real_part = jnp.einsum(
        "fsim,fsjm->sfij", first_spec[0], second_spec[0], preferred_element_type=jnp.float32
    )
    real_part = real_part + jnp.einsum(
        "fsim,fsjm->sfij", first_spec[1], second_spec[1], preferred_element_type=jnp.float32
    )
    imag_part = jnp.einsum(
        "fsim,fsjm->sfij", first_spec[1], second_spec[0], preferred_element_type=jnp.float32
    )
    imag_part = imag_part - jnp.einsum(
        "fsim,fsjm->sfij", first_spec[0], second_spec[1], preferred_element_type=jnp.float32
    )
    common = jnp.einsum("sim,sjm->sij", first_flags, second_flags, precision=lax.Precision.HIGHEST)
    weight = in_use[:, None, None] / jnp.maximum(common, 1.0)
    both = jnp.stack([real_part, imag_part], axis=2) * weight[:, None, None]
    return both.reshape(both.shape[0], both.shape[1], -1).astype(jnp.bfloat16)


def body(records, window_valid, band_low, band_high, pair_counts, partners):
    channels, windows, length = records.shape
    bin_total = length // 2
    readers, slot_count = partners.shape
    bin_share = bin_total // readers
    whitened = whiten(records, window_valid, band_low, band_high)
    arrived = lax.all_to_all(whitened, "chan", split_axis=1, concat_axis=2, tiled=True)
    spectra = arrived.reshape(2, bin_share, readers, channels, windows)
    copies = jnp.broadcast_to(window_valid[None], (readers, channels, windows))
    valid_all = lax.all_to_all(copies, "chan", split_axis=0, concat_axis=0, tiled=True)
    results = []
    for slot_index in range(slot_count):
        partner_ids = partners[:, slot_index]
        picks = partner_ids[:, None] == jnp.arange(readers, dtype=jnp.int32)[None, :]
        partner_spec = jnp.einsum("rq,cfqim->cfrim", picks.astype(jnp.bfloat16), spectra)
        partner_flags = jnp.einsum(
            "rq,qim->rim", picks.astype(jnp.float32), valid_all, precision=lax.Precision.HIGHEST
        )
        in_use = (slot_index < pair_counts).astype(jnp.float32)
        results.append(cross_stack(spectra, partner_spec, valid_all, partner_flags, in_use))
    stacked = jnp.stack(results, axis=1)
    return lax.all_to_all(stacked, "chan", split_axis=0, concat_axis=2, tiled=True)


LANES = 128


def lane_bins(share):
    quarter = share // 4
    group = np.arange(LANES) % share // quarter
    start = group // 2 * 2 * quarter + 2 * (np.arange(LANES) % quarter)
    return start + group % 2, start + 1 - group % 2


def packed_table(length, share, readers):
    quarter = share // 4
    samples = np.arange(length // 2)
    tables = []
    for quad in range(readers // 4):
        for odd in range(2):
            columns = []
            for chunk in (2 * quad, 2 * quad + 1):
                order = (2 * chunk + 1, 2 * chunk) if odd else (2 * chunk, 2 * chunk + 1)
                starts = [t * share + h * share // 2 for h in range(2) for t in order]
                bins = np.concatenate([start + 2 * np.arange(quarter) + odd for start in starts])
                phase = (samples[:, None] * bins[None, :]) % length
                angles = phase.astype(np.float32) * np.float32(2.0 * math.pi / length)
                columns += [np.cos(angles), -np.sin(angles)]
            tables.append(np.concatenate(columns, axis=1))
    return np.stack(tables).reshape(readers // 4, 2, length // 2, 2 * LANES).astype(ml_dtypes.bfloat16)


def packed_band(share):
    even_first, odd_first = lane_bins(share)
    columns = np.concatenate([even_first, share + odd_first])
    front = np.arange(share) // (share // 4) % 2 == 0
    inner = np.concatenate(
        [
            np.where(front, even_first[:share], share + odd_first[:share]),
            np.where(front, share + odd_first[:share], even_first[:share]),
        ]
    )
    rows = np.concatenate([inner - LANES, inner, inner + LANES])
    near = np.abs(rows[:, None] - columns[None, :]) <= SMOOTH
    return near.astype(ml_dtypes.bfloat16)


def packed_fold(share):
    half = share // 2
    folds = []
    for order in lane_bins(share):
        placed = np.tile(order[:half], LANES // half)
        folds.append(np.arange(half)[:, None] == placed[None, :])
    return np.stack([np.concatenate([fold, fold], axis=1) for fold in folds]).astype(
        ml_dtypes.bfloat16
    )


def packed_spread(channels):
    lane = np.arange(LANES) % (channels * channels)
    rows = np.arange(channels)[:, None]
    both = np.concatenate([rows == lane // channels, rows == lane % channels], axis=1)
    return np.concatenate([both] * 3).astype(ml_dtypes.bfloat16)


def fused_kernel(
    n,
    bin_total,
    records_in,
    valid_in,
    low_in,
    high_in,
    counts_in,
    partners_in,
    table,
    band_in,
    fold_in,
    spread_in,
    out,
    records,
    valid,
    low,
    high,
    counts,
    partners,
    band,
    fold,
    spread,
    tables,
    signs,
    spec,
    mags,
    moved,
    send,
    recv,
    valids,
    flags,
    full,
    turned,
    compact,
    stacked,
    state,
    table_sem,
    valid_send,
    valid_recv,
    spec_send,
    spec_recv,
    out_send,
    out_recv,
    in_sem,
):
    me = lax.axis_index("chan")
    channels, windows, length = records.shape
    share = bin_total // n
    rows = channels * windows
    slots = partners.shape[0]
    chunks = n // 2
    quads = n // 4
    samples = length // 2
    half = share // 2
    packed_windows = windows // 2
    packed_rows = rows // 2

    def far_near(count, step):
        return jnp.where(step % 2 == 0, count // 2 + step // 2, count // 2 - 1 - step // 2)

    def peer(step):
        return me ^ step

    barrier = pltpu.get_barrier_semaphore()
    for step in range(1, n):
        pl.semaphore_signal(
            barrier, inc=1, device_id={"chan": peer(step)}, device_id_type=pl.DeviceIdType.MESH
        )

    def table_copy(quad):
        return pltpu.make_async_copy(table.at[quad], tables.at[quad], table_sem.at[quad])

    inputs = [
        pltpu.make_async_copy(source, target, in_sem.at[i])
        for i, (source, target) in enumerate(
            [
                (valid_in, valid),
                (records_in, records),
                (low_in, low),
                (high_in, high),
                (counts_in, counts),
                (partners_in, partners),
                (band_in, band),
                (fold_in, fold),
                (spread_in, spread),
            ]
        )
    ]
    for copy in inputs:
        copy.start()
    half_quads = quads // 2
    for place in [*range(half_quads, quads), *reversed(range(half_quads))]:
        table_copy(place + me // (n // 2) * (quads - 1 - 2 * place)).start()
    for copy in inputs:
        copy.wait()

    valids[me] = valid[...]

    row = lax.broadcasted_iota(jnp.int32, (rows, windows), 0)
    window_lane = lax.broadcasted_iota(jnp.int32, (rows, windows), 1)
    spread_valid = jnp.broadcast_to(valid[...][:, None, :], (channels, windows, windows))
    spread_valid = spread_valid.reshape(rows, windows)
    level = jnp.sum(
        jnp.where(row % windows == window_lane, spread_valid, 0.0), axis=1, keepdims=True
    )
    level = jnp.broadcast_to(level, (rows, LANES)).astype(jnp.bfloat16)

    def to_signs(part, _):
        at = pl.multiple_of(part * LANES, LANES)
        later = pl.multiple_of(samples + part * LANES, LANES)

        def sign(x):
            one = jnp.ones_like(x)
            return jnp.where(x > 0, one, jnp.where(x < 0, -one, jnp.zeros_like(x)))

        a = sign(records[:, :, pl.ds(at, LANES)].reshape(rows, LANES))
        b = sign(records[:, :, pl.ds(later, LANES)].reshape(rows, LANES))
        signs[0, :, pl.ds(at, LANES)] = (a + b) * level
        signs[1, :, pl.ds(at, LANES)] = (a - b) * level
        return 0

    lax.fori_loop(0, samples // LANES, to_signs, 0)

    lane = lax.broadcasted_iota(jnp.int32, (1, LANES), 1)
    first = lane < share
    inner = lane % share
    quarter = share // 4
    front = inner // quarter % 2 == 0
    lower = inner < half

    mags[:, 0:LANES] = jnp.zeros((rows, LANES), jnp.bfloat16)
    mags[:, (chunks + 1) * LANES : (chunks + 2) * LANES] = jnp.zeros((rows, LANES), jnp.bfloat16)

    upper = me // (n // 2)

    def mirrored(place, count):
        return place + upper * (count - 1 - 2 * place)

    def transform(place, _):
        quad = mirrored(place, quads)
        table_copy(quad).wait()
        even = jnp.dot(signs[0], tables[quad, 0], preferred_element_type=jnp.float32)
        odd = jnp.dot(signs[1], tables[quad, 1], preferred_element_type=jnp.float32)
        for part in range(2):
            chunk = 2 * quad + part
            e = even[:, part * LANES : (part + 1) * LANES]
            o = odd[:, part * LANES : (part + 1) * LANES]
            spec[2 * chunk] = jnp.where(front, e, o)
            spec[2 * chunk + 1] = jnp.where(front, o, e)
            e, o = e * e, o * o
            e, o = e + pltpu.roll(e, share, 1), o + pltpu.roll(o, share, 1)
            at = pl.multiple_of((chunk + 1) * LANES, LANES)
            mags[:, pl.ds(at, LANES)] = jnp.sqrt(jnp.where(first, e, o)).astype(jnp.bfloat16)
        return 0

    lax.fori_loop(quads // 2, quads, transform, 0)

    pl.semaphore_wait(barrier, n - 1)

    def valid_copy(source, target):
        return pltpu.make_async_remote_copy(
            src_ref=valids.at[source],
            dst_ref=valids.at[source],
            send_sem=valid_send.at[target],
            recv_sem=valid_recv.at[source],
            device_id={"chan": target},
            device_id_type=pl.DeviceIdType.MESH,
        )

    def spec_copy(part, source, target):
        return pltpu.make_async_remote_copy(
            src_ref=send.at[part, target],
            dst_ref=recv.at[part, source],
            send_sem=spec_send.at[part, target],
            recv_sem=spec_recv.at[part, source],
            device_id={"chan": target},
            device_id_type=pl.DeviceIdType.MESH,
        )

    def out_copy(part, source, target):
        at = pl.multiple_of(source * share + part * half, half)
        return pltpu.make_async_remote_copy(
            src_ref=stacked.at[part, target],
            dst_ref=out.at[:, pl.ds(at, half), :],
            send_sem=out_send.at[part, target],
            recv_sem=out_recv.at[part, source],
            device_id={"chan": target},
            device_id_type=pl.DeviceIdType.MESH,
        )

    channel = lax.broadcasted_iota(jnp.int32, (channels, 1), 0)
    lows = jnp.zeros((channels, 1), jnp.int32)
    highs = jnp.zeros((channels, 1), jnp.int32)
    for c in range(channels):
        lows = jnp.where(channel == c, low[c], lows)
        highs = jnp.where(channel == c, high[c], highs)

    def whiten(chunk):
        at = pl.multiple_of(chunk * LANES, LANES)
        total = jnp.dot(
            mags[:, pl.ds(at, 3 * LANES)], band[...], preferred_element_type=jnp.float32
        )
        for part in range(2):
            target = 2 * chunk + part
            k = target * share + inner // half * half + 2 * (inner % quarter)
            k = k + jnp.where(front, part, 1 - part)
            near = jnp.minimum(k + SMOOTH, bin_total - 1) - jnp.maximum(k - SMOOTH, 0) + 1
            smoothed = total[:, part * LANES : (part + 1) * LANES] * (1.0 / near.astype(jnp.float32))
            inside = jnp.where((k >= lows) & (k < highs), 1.0, 0.0)
            y = spec[target] / jnp.maximum(smoothed, 1.0)
            y = y.reshape(channels, windows, LANES) * inside[:, None, :]
            early = y[:, :packed_windows].reshape(packed_rows, LANES)
            late = y[:, packed_windows:].reshape(packed_rows, LANES)
            send[0, target] = jnp.where(lower, early, pltpu.roll(late, half, 1)).astype(
                jnp.bfloat16
            )
            send[1, target] = jnp.where(lower, pltpu.roll(early, LANES - half, 1), late).astype(
                jnp.bfloat16
            )

    def send_spec(place):
        chunk = mirrored(place, chunks)
        whiten(chunk)
        for part in range(2):
            target = 2 * chunk + part

            @pl.when(target != me)
            def _():
                spec_copy(0, me, target).start()

    inside_far = chunks // 2 - 1

    def send_far(step, _):
        send_spec(chunks // 2 + 1 + (me // 2 + step) % inside_far)
        return 0

    lax.fori_loop(0, inside_far, send_far, 0)

    def send_rest(step, _):
        quad = half_quads - 1 - step
        transform(quad, 0)
        for c in (2, 1):
            send_spec(2 * quad + c)
        return 0

    lax.fori_loop(0, half_quads, send_rest, 0)
    send_spec(0)

    def send_valid(step, _):
        valid_copy(me, me ^ far_near(n, step)).start()
        return 0

    lax.fori_loop(0, n - 1, send_valid, 0)

    def send_later(step, _):
        spec_copy(1, me, me ^ far_near(n, step)).start()
        return 0

    lax.fori_loop(0, n - 1, send_later, 0)

    def place(source, block):
        moved[...] = block.astype(jnp.float32)
        for window in range(packed_windows):
            part = moved[pl.ds(window, channels, stride=packed_windows), :]
            swapped = pltpu.roll(part, share, 1)
            full[source, window * channels : (window + 1) * channels] = part
            turned[source, window * channels : (window + 1) * channels] = jnp.where(
                first, -swapped, swapped
            )

    def spread_flags(source):
        pieces = []
        rest = valids[source]
        for _ in range(3):
            piece = rest.astype(jnp.bfloat16)
            rest = rest - piece.astype(jnp.float32)
            pieces.append(piece)
        flags[source] = lax.dot_general(
            jnp.concatenate(pieces, axis=0),
            spread[...],
            (((0,), (0,)), ((), ())),
            preferred_element_type=jnp.float32,
        )

    spread_flags(me)

    def receive(part, step, _):
        source = me ^ far_near(n, step)
        spec_copy(part, source, me).wait_recv()
        if part == 0:
            valid_copy(source, me).wait_recv()
            spread_flags(source)
        place(source, recv[part, source])
        return 0

    folding = fold[me % 2]

    def order(place_index):
        return me ^ far_near(n, place_index)

    def stack_entry(entry):
        place_index = state[0]
        slot = state[1]
        reader = order(place_index % n)
        partner = partners[slot, reader]

        def window_step(window, totals):
            at = pl.multiple_of(window * channels, channels)
            straight = full[partner, pl.ds(at, channels), :]
            crossed = turned[partner, pl.ds(at, channels), :]
            totals = list(totals)
            for i in range(channels):
                own = full[reader, pl.ds(at + i, 1), :]
                totals[i] += own * straight
                totals[channels + i] += own * crossed
            return tuple(totals)

        zero = jnp.zeros((channels, LANES), jnp.float32)
        totals = lax.fori_loop(0, packed_windows, window_step, (zero,) * (2 * channels), unroll=4)
        tile = jnp.concatenate(totals, axis=0)
        high_part = tile.astype(jnp.bfloat16)
        low_part = (tile - high_part.astype(jnp.float32)).astype(jnp.bfloat16)
        flat = lax.dot_general(
            folding,
            jnp.concatenate([high_part, low_part], axis=1),
            (((1,), (1,)), ((), ())),
            preferred_element_type=jnp.float32,
        )
        common = flags[reader, :, 0:LANES] * flags[partner, :, LANES : 2 * LANES]
        common = jnp.sum(common, axis=0, keepdims=True)
        compact[entry] = (flat * (1.0 / jnp.maximum(common, 1.0))).astype(jnp.bfloat16)
        more = slot + 1 < counts[reader]
        state[0] = jnp.where(more, place_index, place_index + 1)
        state[1] = jnp.where(more, slot + 1, 0)

    entries = 2 * n
    ready = [min(slots * (p + 1), entries - (n - 1 - p)) for p in range(n)]
    added = [now - before for now, before in zip(ready, [0] + ready)]

    def send_stack(part, begin, shift, width, place_index, _):
        for extra in range(width):
            stack_entry(begin + (place_index - shift) * width + extra)
        base = state[2]
        reader = order(place_index)
        count = counts[reader]
        for slot in range(slots):
            block = compact[jnp.minimum(base + slot, entries - 1)]
            stacked[part, reader, slot] = jnp.where(slot < count, block, jnp.zeros_like(block))

        @pl.when(place_index < n - 1)
        def _():
            out_copy(part, me, reader).start()

        state[2] = base + count
        return 0

    for part in range(2):
        place(me, send[part, me])
        lax.fori_loop(0, n - 1, functools.partial(receive, part), 0)
        for i in range(3):
            state[i] = 0
        p = 0
        while p < n:
            stop = p
            while stop < n and added[stop] == added[p]:
                stop += 1
            step = functools.partial(send_stack, part, ready[p] - added[p], p, added[p])
            lax.fori_loop(p, stop, step, 0)
            p = stop
        own_at = pl.multiple_of(me * share + part * half, half)
        out[:, pl.ds(own_at, half), :] = stacked[part, me]

    def finish_copies(step, _):
        target = peer(step)
        valid_copy(me, target).wait_send()
        for part in range(2):
            spec_copy(part, me, target).wait_send()
            out_copy(part, me, target).wait_send()
            out_copy(part, target, me).wait_recv()
        return 0

    lax.fori_loop(1, n, finish_copies, 0)


def fused(n, records, window_valid, band_low, band_high, pair_counts, partners):
    channels, windows, length = records.shape
    bin_total = length // 2
    slots = partners.shape[1]
    share = bin_total // n
    rows = channels * windows
    table = jnp.asarray(packed_table(length, share, n))
    band = jnp.asarray(packed_band(share))
    fold = jnp.asarray(packed_fold(share))
    spread = jnp.asarray(packed_spread(channels))
    hbm = pl.BlockSpec(memory_space=pltpu.HBM)
    dma = pltpu.SemaphoreType.DMA
    by_slot = partners.T
    out = pl.pallas_call(
        functools.partial(fused_kernel, n, bin_total),
        out_shape=pltpu.VMEM((slots, bin_total, LANES), jnp.bfloat16),
        in_specs=[hbm] * 10,
        out_specs=pl.BlockSpec(memory_space=pltpu.VMEM),
        scratch_shapes=[
            pltpu.VMEM(records.shape, jnp.bfloat16),
            pltpu.VMEM(window_valid.shape, jnp.float32),
            pltpu.SMEM(band_low.shape, jnp.int32),
            pltpu.SMEM(band_high.shape, jnp.int32),
            pltpu.SMEM(pair_counts.shape, jnp.int32),
            pltpu.SMEM(by_slot.shape, jnp.int32),
            pltpu.VMEM(band.shape, jnp.bfloat16),
            pltpu.VMEM(fold.shape, jnp.bfloat16),
            pltpu.VMEM(spread.shape, jnp.bfloat16),
            pltpu.VMEM(table.shape, jnp.bfloat16),
            pltpu.VMEM((2, rows, length // 2), jnp.bfloat16),
            pltpu.VMEM((n, rows, LANES), jnp.float32),
            pltpu.VMEM((rows, (n // 2 + 2) * LANES), jnp.bfloat16),
            pltpu.VMEM((rows // 2, LANES), jnp.float32),
            pltpu.VMEM((2, n, rows // 2, LANES), jnp.bfloat16),
            pltpu.VMEM((2, n, rows // 2, LANES), jnp.bfloat16),
            pltpu.VMEM((n, channels, windows), jnp.float32),
            pltpu.VMEM((n, windows, 2 * LANES), jnp.float32),
            pltpu.VMEM((n, rows // 2, LANES), jnp.float32),
            pltpu.VMEM((n, rows // 2, LANES), jnp.float32),
            pltpu.VMEM((2 * n, share // 2, LANES), jnp.bfloat16),
            pltpu.VMEM((2, n, slots, share // 2, LANES), jnp.bfloat16),
            pltpu.SMEM((3,), jnp.int32),
            dma((n // 4,)),
            dma((n,)),
            dma((n,)),
            dma((2, n)),
            dma((2, n)),
            dma((2, n)),
            dma((2, n)),
            dma((9,)),
        ],
        compiler_params=pltpu.CompilerParams(
            collective_id=0, has_side_effects=True, vmem_limit_bytes=60 * 1024 * 1024
        ),
    )(records, window_valid, band_low, band_high, pair_counts, by_slot, table, band, fold, spread)
    return out[None]


def solution(mesh):
    def run(records, window_valid, band_low, band_high, pair_counts, partners):
        n = mesh.shape["chan"]
        channels, windows, length = records.shape
        whole_tiles = 2 * (length // 2 // n) == LANES and 2 * channels * channels == LANES
        args = (records, window_valid, band_low, band_high, pair_counts, partners)
        if whole_tiles and n >= 8 and n & (n - 1) == 0 and windows % 32 == 0:
            return fused(n, *args)
        return body(*args)

    return jax.shard_map(
        run,
        mesh=mesh,
        in_specs=(
            P(("groups", "chan"), None, None),
            P(("groups", "chan"), None),
            P(("groups", "chan")),
            P(("groups", "chan")),
            P("groups"),
            P("groups", None),
        ),
        out_specs=P(("groups", "chan"), None, None, None),
        check_vma=False,
    )
```

```python
import functools
import math

import jax
import jax.numpy as jnp
import ml_dtypes
import numpy as np
from jax import lax
from jax.experimental import pallas as pl
from jax.experimental.pallas import tpu as pltpu
from jax.sharding import PartitionSpec as P

SMOOTH = 8


def dft_table(length, first_bin, bin_count):
    sample_index = lax.broadcasted_iota(jnp.int32, (length, bin_count), 0)
    bin_index = lax.broadcasted_iota(jnp.int32, (length, bin_count), 1) + first_bin
    phase_step = sample_index * bin_index % length
    angles = phase_step.astype(jnp.float32) * (2.0 * math.pi / length)
    return jnp.concatenate([jnp.cos(angles), -jnp.sin(angles)], axis=1).astype(jnp.bfloat16)


def finish(spectrum, band_low, band_high, channels, windows):
    bin_total = spectrum.shape[1]
    magnitude = jnp.sqrt(spectrum[0] * spectrum[0] + spectrum[1] * spectrum[1])
    padded = jnp.pad(magnitude, ((SMOOTH, SMOOTH), (0, 0)))
    summed = padded[0:bin_total]
    for offset in range(1, 2 * SMOOTH + 1):
        summed = summed + padded[offset : offset + bin_total]
    bin_column = lax.broadcasted_iota(jnp.int32, (bin_total, 1), 0)
    in_range = (
        jnp.minimum(bin_column + SMOOTH, bin_total - 1) - jnp.maximum(bin_column - SMOOTH, 0) + 1
    )
    smoothed = summed / in_range.astype(jnp.float32)
    divisor = jnp.maximum(smoothed, 1.0).reshape(bin_total, channels, windows)
    bin_index = lax.broadcasted_iota(jnp.int32, (bin_total, channels, 1), 0)
    inside = (
        (bin_index >= band_low[None, :, None]) & (bin_index < band_high[None, :, None])
    ).astype(jnp.float32)
    shaped = spectrum.reshape(2, bin_total, channels, windows)
    return (
        (shaped / divisor * inside).astype(jnp.bfloat16).reshape(2, bin_total, channels * windows)
    )


def whiten(records, window_valid, band_low, band_high):
    channels, windows, length = records.shape
    bin_total = length // 2
    row_total = channels * windows
    one_bit = (jnp.sign(records.astype(jnp.float32)) * window_valid[:, :, None]).astype(
        jnp.bfloat16
    )
    one_bit = one_bit.reshape(row_total, length)
    blocks = []
    for first_bin in range(0, bin_total, 256):
        dft_block = dft_table(length, first_bin, 256)
        partial_spec = lax.dot_general(
            dft_block, one_bit, (((0,), (1,)), ((), ())), preferred_element_type=jnp.float32
        )
        blocks.append(partial_spec.reshape(2, 256, row_total))
    spectrum = jnp.concatenate(blocks, axis=1)
    return finish(spectrum, band_low, band_high, channels, windows)


def cross_stack(first_spec, second_spec, first_flags, second_flags, in_use):
    real_part = jnp.einsum(
        "fsim,fsjm->sfij", first_spec[0], second_spec[0], preferred_element_type=jnp.float32
    )
    real_part = real_part + jnp.einsum(
        "fsim,fsjm->sfij", first_spec[1], second_spec[1], preferred_element_type=jnp.float32
    )
    imag_part = jnp.einsum(
        "fsim,fsjm->sfij", first_spec[1], second_spec[0], preferred_element_type=jnp.float32
    )
    imag_part = imag_part - jnp.einsum(
        "fsim,fsjm->sfij", first_spec[0], second_spec[1], preferred_element_type=jnp.float32
    )
    common = jnp.einsum("sim,sjm->sij", first_flags, second_flags, precision=lax.Precision.HIGHEST)
    weight = in_use[:, None, None] / jnp.maximum(common, 1.0)
    both = jnp.stack([real_part, imag_part], axis=2) * weight[:, None, None]
    return both.reshape(both.shape[0], both.shape[1], -1).astype(jnp.bfloat16)


def body(records, window_valid, band_low, band_high, pair_counts, partners):
    channels, windows, length = records.shape
    bin_total = length // 2
    readers, slot_count = partners.shape
    bin_share = bin_total // readers
    whitened = whiten(records, window_valid, band_low, band_high)
    arrived = lax.all_to_all(whitened, "chan", split_axis=1, concat_axis=2, tiled=True)
    spectra = arrived.reshape(2, bin_share, readers, channels, windows)
    copies = jnp.broadcast_to(window_valid[None], (readers, channels, windows))
    valid_all = lax.all_to_all(copies, "chan", split_axis=0, concat_axis=0, tiled=True)
    results = []
    for slot_index in range(slot_count):
        partner_ids = partners[:, slot_index]
        picks = partner_ids[:, None] == jnp.arange(readers, dtype=jnp.int32)[None, :]
        partner_spec = jnp.einsum("rq,cfqim->cfrim", picks.astype(jnp.bfloat16), spectra)
        partner_flags = jnp.einsum(
            "rq,qim->rim", picks.astype(jnp.float32), valid_all, precision=lax.Precision.HIGHEST
        )
        in_use = (slot_index < pair_counts).astype(jnp.float32)
        results.append(cross_stack(spectra, partner_spec, valid_all, partner_flags, in_use))
    stacked = jnp.stack(results, axis=1)
    return lax.all_to_all(stacked, "chan", split_axis=0, concat_axis=2, tiled=True)


LANES = 128
FLAG_ROWS = 16


def lane_bins(share):
    quarter = share // 4
    group = np.arange(LANES) % share // quarter
    start = group // 2 * 2 * quarter + 2 * (np.arange(LANES) % quarter)
    return start + group % 2, start + 1 - group % 2


def packed_table(length, share, readers):
    quarter = share // 4
    samples = np.arange(length // 2)
    tables = []
    for quad in range(readers // 4):
        for odd in range(2):
            columns = []
            for chunk in (2 * quad, 2 * quad + 1):
                order = (2 * chunk + 1, 2 * chunk) if odd else (2 * chunk, 2 * chunk + 1)
                starts = [t * share + h * share // 2 for h in range(2) for t in order]
                bins = np.concatenate([start + 2 * np.arange(quarter) + odd for start in starts])
                phase = (samples[:, None] * bins[None, :]) % length
                angles = phase.astype(np.float32) * np.float32(2.0 * math.pi / length)
                columns += [np.cos(angles), -np.sin(angles)]
            tables.append(np.concatenate(columns, axis=1))
    return np.stack(tables).reshape(readers // 4, 2, length // 2, 2 * LANES).astype(ml_dtypes.bfloat16)


def packed_band(share):
    even_first, odd_first = lane_bins(share)
    columns = np.concatenate([even_first, share + odd_first])
    front = np.arange(share) // (share // 4) % 2 == 0
    inner = np.concatenate(
        [
            np.where(front, even_first[:share], share + odd_first[:share]),
            np.where(front, share + odd_first[:share], even_first[:share]),
        ]
    )
    rows = np.concatenate([inner - LANES, inner, inner + LANES])
    near = np.abs(rows[:, None] - columns[None, :]) <= SMOOTH
    return near.astype(ml_dtypes.bfloat16)


def packed_fold(share):
    half = share // 2
    folds = []
    for order in lane_bins(share):
        placed = np.tile(order[:half], LANES // half)
        folds.append(np.arange(half)[:, None] == placed[None, :])
    return np.stack([np.concatenate([fold, fold], axis=1) for fold in folds]).astype(
        ml_dtypes.bfloat16
    )


def packed_spread(channels):
    lane = np.arange(LANES) % (channels * channels)
    rows = np.arange(channels)[:, None]
    both = np.concatenate([rows == lane // channels, rows == lane % channels], axis=1)
    unused = np.zeros((FLAG_ROWS - channels, 2 * LANES), bool)
    return np.concatenate([both, unused]).astype(ml_dtypes.bfloat16)


def fused_kernel(
    n,
    bin_total,
    records_in,
    valid_in,
    low_in,
    high_in,
    counts_in,
    partners_in,
    table,
    band_in,
    fold_in,
    spread_in,
    out,
    records,
    valid,
    low,
    high,
    counts,
    partners,
    band,
    fold,
    spread,
    tables,
    signs,
    spec,
    mags,
    moved,
    send,
    recv,
    flags,
    full,
    turned,
    compact,
    stacked,
    state,
    table_sem,
    spec_send,
    spec_recv,
    out_send,
    out_recv,
    in_sem,
):
    me = lax.axis_index("chan")
    channels, windows, length = records.shape
    share = bin_total // n
    rows = channels * windows
    slots = partners.shape[0]
    chunks = n // 2
    quads = n // 4
    samples = length // 2
    half = share // 2
    packed_windows = windows // 2
    packed_rows = rows // 2
    heights = (packed_rows + FLAG_ROWS, packed_rows)

    def far_near(count, step):
        return jnp.where(step % 2 == 0, count // 2 + step // 2, count // 2 - 1 - step // 2)

    def peer(step):
        return me ^ step

    barrier = pltpu.get_barrier_semaphore()
    def table_copy(quad):
        return pltpu.make_async_copy(table.at[quad], tables.at[quad], table_sem.at[quad])

    inputs = [
        pltpu.make_async_copy(source, target, in_sem.at[i])
        for i, (source, target) in enumerate(
            [
                (valid_in, valid),
                (records_in, records),
                (low_in, low),
                (high_in, high),
                (counts_in, counts),
                (partners_in, partners),
                (band_in, band),
                (fold_in, fold),
                (spread_in, spread),
            ]
        )
    ]
    for copy in inputs:
        copy.start()
    for place in reversed(range(quads)):
        table_copy(place + me // (n // 2) * (quads - 1 - 2 * place)).start()
    for step in range(1, n):
        pl.semaphore_signal(
            barrier, inc=1, device_id={"chan": peer(step)}, device_id_type=pl.DeviceIdType.MESH
        )
    for copy in inputs:
        copy.wait()

    pieces = []
    rest = valid[...]
    for _ in range(3):
        piece = rest.astype(jnp.bfloat16).astype(jnp.float32)
        rest = rest - piece
        pieces.append(piece)
    unused = jnp.zeros((channels, LANES - 3 * windows), jnp.float32)
    pieces = jnp.concatenate(pieces + [unused], axis=1)
    pieces = jnp.concatenate([pieces, jnp.zeros((FLAG_ROWS - channels, LANES), jnp.float32)], axis=0)
    for target in range(n):
        send[0, target, rows // 2 : rows // 2 + FLAG_ROWS] = pieces.astype(jnp.bfloat16)

    row = lax.broadcasted_iota(jnp.int32, (rows, windows), 0)
    window_lane = lax.broadcasted_iota(jnp.int32, (rows, windows), 1)
    spread_valid = jnp.broadcast_to(valid[...][:, None, :], (channels, windows, windows))
    spread_valid = spread_valid.reshape(rows, windows)
    level = jnp.sum(
        jnp.where(row % windows == window_lane, spread_valid, 0.0), axis=1, keepdims=True
    )
    level = jnp.broadcast_to(level, (rows, LANES)).astype(jnp.bfloat16)

    def to_signs(part, _):
        at = pl.multiple_of(part * LANES, LANES)
        later = pl.multiple_of(samples + part * LANES, LANES)

        def sign(x):
            one = jnp.ones_like(x)
            return jnp.where(x > 0, one, jnp.where(x < 0, -one, jnp.zeros_like(x)))

        a = sign(records[:, :, pl.ds(at, LANES)].reshape(rows, LANES))
        b = sign(records[:, :, pl.ds(later, LANES)].reshape(rows, LANES))
        signs[0, :, pl.ds(at, LANES)] = (a + b) * level
        signs[1, :, pl.ds(at, LANES)] = (a - b) * level
        return 0

    lax.fori_loop(0, samples // LANES, to_signs, 0)

    lane = lax.broadcasted_iota(jnp.int32, (1, LANES), 1)
    first = lane < share
    inner = lane % share
    quarter = share // 4
    front = inner // quarter % 2 == 0
    lower = inner < half

    mags[:, 0:LANES] = jnp.zeros((rows, LANES), jnp.bfloat16)
    mags[:, (chunks + 1) * LANES : (chunks + 2) * LANES] = jnp.zeros((rows, LANES), jnp.bfloat16)

    upper = me // (n // 2)

    def mirrored(place, count):
        return place + upper * (count - 1 - 2 * place)

    def transform(place, _):
        quad = mirrored(place, quads)
        table_copy(quad).wait()
        even = jnp.dot(signs[0], tables[quad, 0], preferred_element_type=jnp.float32)
        odd = jnp.dot(signs[1], tables[quad, 1], preferred_element_type=jnp.float32)
        for part in range(2):
            chunk = 2 * quad + part
            e = even[:, part * LANES : (part + 1) * LANES]
            o = odd[:, part * LANES : (part + 1) * LANES]
            spec[2 * chunk] = jnp.where(front, e, o)
            spec[2 * chunk + 1] = jnp.where(front, o, e)
            e, o = e * e, o * o
            e, o = e + pltpu.roll(e, share, 1), o + pltpu.roll(o, share, 1)
            at = pl.multiple_of((chunk + 1) * LANES, LANES)
            mags[:, pl.ds(at, LANES)] = jnp.sqrt(jnp.where(first, e, o)).astype(jnp.bfloat16)
        return 0

    transform(quads - 1, 0)

    pl.semaphore_wait(barrier, n - 1)

    def spec_copy(part, source, target):
        return pltpu.make_async_remote_copy(
            src_ref=send.at[part, target, pl.ds(0, heights[part])],
            dst_ref=recv.at[part, source, pl.ds(0, heights[part])],
            send_sem=spec_send.at[part, target],
            recv_sem=spec_recv.at[part, source],
            device_id={"chan": target},
            device_id_type=pl.DeviceIdType.MESH,
        )

    def out_copy(part, source, target):
        at = pl.multiple_of(source * share + part * half, half)
        return pltpu.make_async_remote_copy(
            src_ref=stacked.at[part, target],
            dst_ref=out.at[:, pl.ds(at, half), :],
            send_sem=out_send.at[part, target],
            recv_sem=out_recv.at[part, source],
            device_id={"chan": target},
            device_id_type=pl.DeviceIdType.MESH,
        )

    channel = lax.broadcasted_iota(jnp.int32, (channels, 1), 0)
    lows = jnp.zeros((channels, 1), jnp.int32)
    highs = jnp.zeros((channels, 1), jnp.int32)
    for c in range(channels):
        lows = jnp.where(channel == c, low[c], lows)
        highs = jnp.where(channel == c, high[c], highs)

    def whiten(chunk):
        at = pl.multiple_of(chunk * LANES, LANES)
        total = jnp.dot(
            mags[:, pl.ds(at, 3 * LANES)], band[...], preferred_element_type=jnp.float32
        )
        for part in range(2):
            target = 2 * chunk + part
            k = target * share + inner // half * half + 2 * (inner % quarter)
            k = k + jnp.where(front, part, 1 - part)
            near = jnp.minimum(k + SMOOTH, bin_total - 1) - jnp.maximum(k - SMOOTH, 0) + 1
            smoothed = total[:, part * LANES : (part + 1) * LANES] * (1.0 / near.astype(jnp.float32))
            inside = jnp.where((k >= lows) & (k < highs), 1.0, 0.0)
            y = spec[target] / jnp.maximum(smoothed, 1.0)
            y = y.reshape(channels, windows, LANES) * inside[:, None, :]
            early = y[:, :packed_windows].reshape(packed_rows, LANES)
            late = y[:, packed_windows:].reshape(packed_rows, LANES)
            send[0, target, 0:packed_rows] = jnp.where(lower, early, pltpu.roll(late, half, 1)).astype(
                jnp.bfloat16
            )
            send[1, target, 0:packed_rows] = jnp.where(lower, pltpu.roll(early, LANES - half, 1), late).astype(
                jnp.bfloat16
            )

    def send_spec(place):
        chunk = mirrored(place, chunks)
        whiten(chunk)
        for part in range(2):
            target = 2 * chunk + part

            @pl.when(target != me)
            def _():
                spec_copy(0, me, target).start()

    send_spec(chunks - 1)

    def send_rest(step, _):
        quad = quads - 2 - step
        transform(quad, 0)
        for c in (2, 1):
            send_spec(2 * quad + c)
        return 0

    lax.fori_loop(0, quads - 1, send_rest, 0)
    send_spec(0)

    def send_later(step, _):
        spec_copy(1, me, me ^ far_near(n, step)).start()
        return 0

    lax.fori_loop(0, n - 1, send_later, 0)

    def place(source, block):
        moved[...] = block.astype(jnp.float32)
        for window in range(packed_windows):
            part = moved[pl.ds(window, channels, stride=packed_windows), :]
            swapped = pltpu.roll(part, share, 1)
            full[source, window * channels : (window + 1) * channels] = part
            turned[source, window * channels : (window + 1) * channels] = jnp.where(
                first, -swapped, swapped
            )

    def spread_flags(source, block):
        spreads = lax.dot_general(
            block, spread[...], (((0,), (0,)), ((), ())), preferred_element_type=jnp.float32
        )
        flags[source] = (
            spreads[:windows] + spreads[windows : 2 * windows] + spreads[2 * windows : 3 * windows]
        )

    flag_rows = slice(rows // 2, rows // 2 + FLAG_ROWS)
    spread_flags(me, send[0, me, flag_rows])

    def receive(part, step, _):
        source = me ^ far_near(n, step)
        spec_copy(part, source, me).wait_recv()
        if part == 0:
            spread_flags(source, recv[0, source, flag_rows])
        place(source, recv[part, source, 0:packed_rows])
        return 0

    folding = fold[me % 2]

    def order(place_index):
        return me ^ far_near(n, place_index)

    def stack_entry(entry):
        place_index = state[0]
        slot = state[1]
        reader = order(place_index % n)
        partner = partners[slot, reader]

        def window_step(window, totals):
            at = pl.multiple_of(window * channels, channels)
            straight = full[partner, pl.ds(at, channels), :]
            crossed = turned[partner, pl.ds(at, channels), :]
            totals = list(totals)
            for i in range(channels):
                own = full[reader, pl.ds(at + i, 1), :]
                totals[i] += own * straight
                totals[channels + i] += own * crossed
            return tuple(totals)

        zero = jnp.zeros((channels, LANES), jnp.float32)
        totals = lax.fori_loop(0, packed_windows, window_step, (zero,) * (2 * channels), unroll=4)
        tile = jnp.concatenate(totals, axis=0)
        high_part = tile.astype(jnp.bfloat16)
        low_part = (tile - high_part.astype(jnp.float32)).astype(jnp.bfloat16)
        flat = lax.dot_general(
            folding,
            jnp.concatenate([high_part, low_part], axis=1),
            (((1,), (1,)), ((), ())),
            preferred_element_type=jnp.float32,
        )
        common = flags[reader, :, 0:LANES] * flags[partner, :, LANES : 2 * LANES]
        common = jnp.sum(common, axis=0, keepdims=True)
        compact[entry] = (flat * (1.0 / jnp.maximum(common, 1.0))).astype(jnp.bfloat16)
        more = slot + 1 < counts[reader]
        state[0] = jnp.where(more, place_index, place_index + 1)
        state[1] = jnp.where(more, slot + 1, 0)

    entries = 2 * n
    ready = [min(slots * (p + 1), entries - (n - 1 - p)) for p in range(n)]
    added = [now - before for now, before in zip(ready, [0] + ready)]

    def send_stack(part, begin, shift, width, place_index, _):
        for extra in range(width):
            stack_entry(begin + (place_index - shift) * width + extra)
        base = state[2]
        reader = order(place_index)
        count = counts[reader]
        for slot in range(slots):
            block = compact[jnp.minimum(base + slot, entries - 1)]
            stacked[part, reader, slot] = jnp.where(slot < count, block, jnp.zeros_like(block))

        @pl.when(place_index < n - 1)
        def _():
            out_copy(part, me, reader).start()

        state[2] = base + count
        return 0

    for part in range(2):
        place(me, send[part, me, 0:packed_rows])
        lax.fori_loop(0, n - 1, functools.partial(receive, part), 0)
        for i in range(3):
            state[i] = 0
        p = 0
        while p < n:
            stop = p
            while stop < n and added[stop] == added[p]:
                stop += 1
            step = functools.partial(send_stack, part, ready[p] - added[p], p, added[p])
            lax.fori_loop(p, stop, step, 0)
            p = stop
        own_at = pl.multiple_of(me * share + part * half, half)
        out[:, pl.ds(own_at, half), :] = stacked[part, me]

    def finish_sends(step, _):
        target = peer(step)
        for part in range(2):
            spec_copy(part, me, target).wait_send()
        out_copy(0, me, target).wait_send()
        return 0

    def finish_copies(part, step, _):
        if part == 1:
            out_copy(1, me, peer(step)).wait_send()
        out_copy(part, peer(step), me).wait_recv()
        return 0

    lax.fori_loop(1, n, finish_sends, 0)
    for part in range(2):
        lax.fori_loop(1, n, functools.partial(finish_copies, part), 0)


def fused(n, records, window_valid, band_low, band_high, pair_counts, partners):
    channels, windows, length = records.shape
    bin_total = length // 2
    slots = partners.shape[1]
    share = bin_total // n
    rows = channels * windows
    table = jnp.asarray(packed_table(length, share, n))
    band = jnp.asarray(packed_band(share))
    fold = jnp.asarray(packed_fold(share))
    spread = jnp.asarray(packed_spread(channels))
    hbm = pl.BlockSpec(memory_space=pltpu.HBM)
    dma = pltpu.SemaphoreType.DMA
    by_slot = partners.T
    out = pl.pallas_call(
        functools.partial(fused_kernel, n, bin_total),
        out_shape=pltpu.VMEM((slots, bin_total, LANES), jnp.bfloat16),
        in_specs=[hbm] * 10,
        out_specs=pl.BlockSpec(memory_space=pltpu.VMEM),
        scratch_shapes=[
            pltpu.VMEM(records.shape, jnp.bfloat16),
            pltpu.VMEM(window_valid.shape, jnp.float32),
            pltpu.SMEM(band_low.shape, jnp.int32),
            pltpu.SMEM(band_high.shape, jnp.int32),
            pltpu.SMEM(pair_counts.shape, jnp.int32),
            pltpu.SMEM(by_slot.shape, jnp.int32),
            pltpu.VMEM(band.shape, jnp.bfloat16),
            pltpu.VMEM(fold.shape, jnp.bfloat16),
            pltpu.VMEM(spread.shape, jnp.bfloat16),
            pltpu.VMEM(table.shape, jnp.bfloat16),
            pltpu.VMEM((2, rows, length // 2), jnp.bfloat16),
            pltpu.VMEM((n, rows, LANES), jnp.float32),
            pltpu.VMEM((rows, (n // 2 + 2) * LANES), jnp.bfloat16),
            pltpu.VMEM((rows // 2, LANES), jnp.float32),
            pltpu.VMEM((2, n, rows // 2 + FLAG_ROWS, LANES), jnp.bfloat16),
            pltpu.VMEM((2, n, rows // 2 + FLAG_ROWS, LANES), jnp.bfloat16),
            pltpu.VMEM((n, windows, 2 * LANES), jnp.float32),
            pltpu.VMEM((n, rows // 2, LANES), jnp.float32),
            pltpu.VMEM((n, rows // 2, LANES), jnp.float32),
            pltpu.VMEM((2 * n, share // 2, LANES), jnp.bfloat16),
            pltpu.VMEM((2, n, slots, share // 2, LANES), jnp.bfloat16),
            pltpu.SMEM((3,), jnp.int32),
            dma((n // 4,)),
            dma((2, n)),
            dma((2, n)),
            dma((2, n)),
            dma((2, n)),
            dma((9,)),
        ],
        compiler_params=pltpu.CompilerParams(
            collective_id=0, has_side_effects=True, vmem_limit_bytes=60 * 1024 * 1024
        ),
    )(records, window_valid, band_low, band_high, pair_counts, by_slot, table, band, fold, spread)
    return out[None]


def solution(mesh):
    def run(records, window_valid, band_low, band_high, pair_counts, partners):
        n = mesh.shape["chan"]
        channels, windows, length = records.shape
        whole_tiles = 2 * (length // 2 // n) == LANES and 2 * channels * channels == LANES
        args = (records, window_valid, band_low, band_high, pair_counts, partners)
        if whole_tiles and n >= 8 and n & (n - 1) == 0 and windows == 32:
            return fused(n, *args)
        return body(*args)

    return jax.shard_map(
        run,
        mesh=mesh,
        in_specs=(
            P(("groups", "chan"), None, None),
            P(("groups", "chan"), None),
            P(("groups", "chan")),
            P(("groups", "chan")),
            P("groups"),
            P("groups", None),
        ),
        out_specs=P(("groups", "chan"), None, None, None),
        check_vma=False,
    )
```

```python
import functools
import math

import jax
import jax.numpy as jnp
import ml_dtypes
import numpy as np
from jax import lax
from jax.experimental import pallas as pl
from jax.experimental.pallas import tpu as pltpu
from jax.sharding import PartitionSpec as P

SMOOTH = 8


def dft_table(length, first_bin, bin_count):
    sample_index = lax.broadcasted_iota(jnp.int32, (length, bin_count), 0)
    bin_index = lax.broadcasted_iota(jnp.int32, (length, bin_count), 1) + first_bin
    phase_step = sample_index * bin_index % length
    angles = phase_step.astype(jnp.float32) * (2.0 * math.pi / length)
    return jnp.concatenate([jnp.cos(angles), -jnp.sin(angles)], axis=1).astype(jnp.bfloat16)


def finish(spectrum, band_low, band_high, channels, windows):
    bin_total = spectrum.shape[1]
    magnitude = jnp.sqrt(spectrum[0] * spectrum[0] + spectrum[1] * spectrum[1])
    padded = jnp.pad(magnitude, ((SMOOTH, SMOOTH), (0, 0)))
    summed = padded[0:bin_total]
    for offset in range(1, 2 * SMOOTH + 1):
        summed = summed + padded[offset : offset + bin_total]
    bin_column = lax.broadcasted_iota(jnp.int32, (bin_total, 1), 0)
    in_range = (
        jnp.minimum(bin_column + SMOOTH, bin_total - 1) - jnp.maximum(bin_column - SMOOTH, 0) + 1
    )
    smoothed = summed / in_range.astype(jnp.float32)
    divisor = jnp.maximum(smoothed, 1.0).reshape(bin_total, channels, windows)
    bin_index = lax.broadcasted_iota(jnp.int32, (bin_total, channels, 1), 0)
    inside = (
        (bin_index >= band_low[None, :, None]) & (bin_index < band_high[None, :, None])
    ).astype(jnp.float32)
    shaped = spectrum.reshape(2, bin_total, channels, windows)
    return (
        (shaped / divisor * inside).astype(jnp.bfloat16).reshape(2, bin_total, channels * windows)
    )


def whiten(records, window_valid, band_low, band_high):
    channels, windows, length = records.shape
    bin_total = length // 2
    row_total = channels * windows
    one_bit = (jnp.sign(records.astype(jnp.float32)) * window_valid[:, :, None]).astype(
        jnp.bfloat16
    )
    one_bit = one_bit.reshape(row_total, length)
    blocks = []
    for first_bin in range(0, bin_total, 256):
        dft_block = dft_table(length, first_bin, 256)
        partial_spec = lax.dot_general(
            dft_block, one_bit, (((0,), (1,)), ((), ())), preferred_element_type=jnp.float32
        )
        blocks.append(partial_spec.reshape(2, 256, row_total))
    spectrum = jnp.concatenate(blocks, axis=1)
    return finish(spectrum, band_low, band_high, channels, windows)


def cross_stack(first_spec, second_spec, first_flags, second_flags, in_use):
    real_part = jnp.einsum(
        "fsim,fsjm->sfij", first_spec[0], second_spec[0], preferred_element_type=jnp.float32
    )
    real_part = real_part + jnp.einsum(
        "fsim,fsjm->sfij", first_spec[1], second_spec[1], preferred_element_type=jnp.float32
    )
    imag_part = jnp.einsum(
        "fsim,fsjm->sfij", first_spec[1], second_spec[0], preferred_element_type=jnp.float32
    )
    imag_part = imag_part - jnp.einsum(
        "fsim,fsjm->sfij", first_spec[0], second_spec[1], preferred_element_type=jnp.float32
    )
    common = jnp.einsum("sim,sjm->sij", first_flags, second_flags, precision=lax.Precision.HIGHEST)
    weight = in_use[:, None, None] / jnp.maximum(common, 1.0)
    both = jnp.stack([real_part, imag_part], axis=2) * weight[:, None, None]
    return both.reshape(both.shape[0], both.shape[1], -1).astype(jnp.bfloat16)


def body(records, window_valid, band_low, band_high, pair_counts, partners):
    channels, windows, length = records.shape
    bin_total = length // 2
    readers, slot_count = partners.shape
    bin_share = bin_total // readers
    whitened = whiten(records, window_valid, band_low, band_high)
    arrived = lax.all_to_all(whitened, "chan", split_axis=1, concat_axis=2, tiled=True)
    spectra = arrived.reshape(2, bin_share, readers, channels, windows)
    copies = jnp.broadcast_to(window_valid[None], (readers, channels, windows))
    valid_all = lax.all_to_all(copies, "chan", split_axis=0, concat_axis=0, tiled=True)
    results = []
    for slot_index in range(slot_count):
        partner_ids = partners[:, slot_index]
        picks = partner_ids[:, None] == jnp.arange(readers, dtype=jnp.int32)[None, :]
        partner_spec = jnp.einsum("rq,cfqim->cfrim", picks.astype(jnp.bfloat16), spectra)
        partner_flags = jnp.einsum(
            "rq,qim->rim", picks.astype(jnp.float32), valid_all, precision=lax.Precision.HIGHEST
        )
        in_use = (slot_index < pair_counts).astype(jnp.float32)
        results.append(cross_stack(spectra, partner_spec, valid_all, partner_flags, in_use))
    stacked = jnp.stack(results, axis=1)
    return lax.all_to_all(stacked, "chan", split_axis=0, concat_axis=2, tiled=True)


LANES = 128
FLAG_ROWS = 16


def lane_bins(share):
    quarter = share // 4
    group = np.arange(LANES) % share // quarter
    start = group // 2 * 2 * quarter + 2 * (np.arange(LANES) % quarter)
    return start + group % 2, start + 1 - group % 2


def packed_table(length, share, readers):
    quarter = share // 4
    samples = np.arange(length // 2)
    tables = []
    for quad in range(readers // 4):
        for odd in range(2):
            columns = []
            for chunk in (2 * quad, 2 * quad + 1):
                order = (2 * chunk + 1, 2 * chunk) if odd else (2 * chunk, 2 * chunk + 1)
                starts = [t * share + h * share // 2 for h in range(2) for t in order]
                bins = np.concatenate([start + 2 * np.arange(quarter) + odd for start in starts])
                phase = (samples[:, None] * bins[None, :]) % length
                angles = phase.astype(np.float32) * np.float32(2.0 * math.pi / length)
                columns += [np.cos(angles), -np.sin(angles)]
            tables.append(np.concatenate(columns, axis=1))
    return np.stack(tables).reshape(readers // 4, 2, length // 2, 2 * LANES).astype(ml_dtypes.bfloat16)


def packed_band(share):
    even_first, odd_first = lane_bins(share)
    columns = np.concatenate([even_first, share + odd_first])
    front = np.arange(share) // (share // 4) % 2 == 0
    inner = np.concatenate(
        [
            np.where(front, even_first[:share], share + odd_first[:share]),
            np.where(front, share + odd_first[:share], even_first[:share]),
        ]
    )
    rows = np.concatenate([inner - LANES, inner, inner + LANES])
    near = np.abs(rows[:, None] - columns[None, :]) <= SMOOTH
    return near.astype(ml_dtypes.bfloat16)


def packed_fold(share):
    half = share // 2
    folds = []
    for order in lane_bins(share):
        placed = np.tile(order[:half], LANES // half)
        folds.append(np.arange(half)[:, None] == placed[None, :])
    return np.stack([np.concatenate([fold, fold], axis=1) for fold in folds]).astype(
        ml_dtypes.bfloat16
    )


def packed_spread(channels):
    lane = np.arange(LANES) % (channels * channels)
    rows = np.arange(channels)[:, None]
    both = np.concatenate([rows == lane // channels, rows == lane % channels], axis=1)
    unused = np.zeros((FLAG_ROWS - channels, 2 * LANES), bool)
    return np.concatenate([both, unused]).astype(ml_dtypes.bfloat16)


def fused_kernel(
    n,
    bin_total,
    records_in,
    valid_in,
    low_in,
    high_in,
    counts_in,
    partners_in,
    table,
    band_in,
    fold_in,
    spread_in,
    out,
    records,
    valid,
    low,
    high,
    counts,
    partners,
    band,
    fold,
    spread,
    tables,
    signs,
    spec,
    mags,
    moved,
    send,
    recv,
    flags,
    full,
    turned,
    compact,
    stacked,
    state,
    table_sem,
    spec_send,
    spec_recv,
    out_send,
    out_recv,
    in_sem,
):
    me = lax.axis_index("chan")
    channels, windows, length = records.shape
    share = bin_total // n
    rows = channels * windows
    slots = partners.shape[0]
    chunks = n // 2
    quads = n // 4
    samples = length // 2
    half = share // 2
    packed_windows = windows // 2
    packed_rows = rows // 2
    heights = (packed_rows + FLAG_ROWS, packed_rows)

    def far_near(count, step):
        k = step // 2
        return jnp.where(step % 2 == 0, count // 2 + (k ^ 2), count // 2 - 1 - k)

    def peer(step):
        return me ^ step

    barrier = pltpu.get_barrier_semaphore()
    def table_copy(quad):
        return pltpu.make_async_copy(table.at[quad], tables.at[quad], table_sem.at[quad])

    inputs = [
        pltpu.make_async_copy(source, target, in_sem.at[i])
        for i, (source, target) in enumerate(
            [
                (valid_in, valid),
                (records_in, records),
                (low_in, low),
                (high_in, high),
                (counts_in, counts),
                (partners_in, partners),
                (band_in, band),
                (fold_in, fold),
                (spread_in, spread),
            ]
        )
    ]
    for copy in inputs:
        copy.start()
    for place in reversed(range(quads)):
        table_copy(place + me // (n // 2) * (quads - 1 - 2 * place)).start()
    for step in range(1, n):
        pl.semaphore_signal(
            barrier, inc=1, device_id={"chan": peer(step)}, device_id_type=pl.DeviceIdType.MESH
        )
    for copy in inputs:
        copy.wait()

    pieces = []
    rest = valid[...]
    for _ in range(3):
        piece = rest.astype(jnp.bfloat16).astype(jnp.float32)
        rest = rest - piece
        pieces.append(piece)
    unused = jnp.zeros((channels, LANES - 3 * windows), jnp.float32)
    pieces = jnp.concatenate(pieces + [unused], axis=1)
    pieces = jnp.concatenate([pieces, jnp.zeros((FLAG_ROWS - channels, LANES), jnp.float32)], axis=0)
    for target in range(n):
        send[0, target, rows // 2 : rows // 2 + FLAG_ROWS] = pieces.astype(jnp.bfloat16)

    row = lax.broadcasted_iota(jnp.int32, (rows, windows), 0)
    window_lane = lax.broadcasted_iota(jnp.int32, (rows, windows), 1)
    spread_valid = jnp.broadcast_to(valid[...][:, None, :], (channels, windows, windows))
    spread_valid = spread_valid.reshape(rows, windows)
    level = jnp.sum(
        jnp.where(row % windows == window_lane, spread_valid, 0.0), axis=1, keepdims=True
    )
    level = jnp.broadcast_to(level, (rows, LANES)).astype(jnp.bfloat16)

    def to_signs(part, _):
        at = pl.multiple_of(part * LANES, LANES)
        later = pl.multiple_of(samples + part * LANES, LANES)

        def sign(x):
            one = jnp.ones_like(x)
            return jnp.where(x > 0, one, jnp.where(x < 0, -one, jnp.zeros_like(x)))

        a = sign(records[:, :, pl.ds(at, LANES)].reshape(rows, LANES))
        b = sign(records[:, :, pl.ds(later, LANES)].reshape(rows, LANES))
        signs[0, :, pl.ds(at, LANES)] = (a + b) * level
        signs[1, :, pl.ds(at, LANES)] = (a - b) * level
        return 0

    lax.fori_loop(0, samples // LANES, to_signs, 0)

    lane = lax.broadcasted_iota(jnp.int32, (1, LANES), 1)
    first = lane < share
    inner = lane % share
    quarter = share // 4
    front = inner // quarter % 2 == 0
    lower = inner < half

    mags[:, 0:LANES] = jnp.zeros((rows, LANES), jnp.bfloat16)
    mags[:, (chunks + 1) * LANES : (chunks + 2) * LANES] = jnp.zeros((rows, LANES), jnp.bfloat16)

    upper = me // (n // 2)

    def mirrored(place, count):
        return place + upper * (count - 1 - 2 * place)

    def transform(place, _):
        quad = mirrored(place, quads)
        table_copy(quad).wait()
        even = jnp.dot(signs[0], tables[quad, 0], preferred_element_type=jnp.float32)
        odd = jnp.dot(signs[1], tables[quad, 1], preferred_element_type=jnp.float32)
        for part in range(2):
            chunk = 2 * quad + part
            e = even[:, part * LANES : (part + 1) * LANES]
            o = odd[:, part * LANES : (part + 1) * LANES]
            spec[2 * chunk] = jnp.where(front, e, o)
            spec[2 * chunk + 1] = jnp.where(front, o, e)
            e, o = e * e, o * o
            e, o = e + pltpu.roll(e, share, 1), o + pltpu.roll(o, share, 1)
            at = pl.multiple_of((chunk + 1) * LANES, LANES)
            mags[:, pl.ds(at, LANES)] = jnp.sqrt(jnp.where(first, e, o)).astype(jnp.bfloat16)
        return 0

    transform(quads - 1, 0)

    pl.semaphore_wait(barrier, n - 1)

    def spec_copy(part, source, target):
        return pltpu.make_async_remote_copy(
            src_ref=send.at[part, target, pl.ds(0, heights[part])],
            dst_ref=recv.at[part, source, pl.ds(0, heights[part])],
            send_sem=spec_send.at[part, target],
            recv_sem=spec_recv.at[part, source],
            device_id={"chan": target},
            device_id_type=pl.DeviceIdType.MESH,
        )

    def out_copy(part, source, target):
        at = pl.multiple_of(source * share + part * half, half)
        return pltpu.make_async_remote_copy(
            src_ref=stacked.at[part, target],
            dst_ref=out.at[:, pl.ds(at, half), :],
            send_sem=out_send.at[part, target],
            recv_sem=out_recv.at[part, source],
            device_id={"chan": target},
            device_id_type=pl.DeviceIdType.MESH,
        )

    channel = lax.broadcasted_iota(jnp.int32, (channels, 1), 0)
    lows = jnp.zeros((channels, 1), jnp.int32)
    highs = jnp.zeros((channels, 1), jnp.int32)
    for c in range(channels):
        lows = jnp.where(channel == c, low[c], lows)
        highs = jnp.where(channel == c, high[c], highs)

    def whiten(chunk):
        at = pl.multiple_of(chunk * LANES, LANES)
        total = jnp.dot(
            mags[:, pl.ds(at, 3 * LANES)], band[...], preferred_element_type=jnp.float32
        )
        for part in range(2):
            target = 2 * chunk + part
            k = target * share + inner // half * half + 2 * (inner % quarter)
            k = k + jnp.where(front, part, 1 - part)
            near = jnp.minimum(k + SMOOTH, bin_total - 1) - jnp.maximum(k - SMOOTH, 0) + 1
            smoothed = total[:, part * LANES : (part + 1) * LANES] * (1.0 / near.astype(jnp.float32))
            inside = jnp.where((k >= lows) & (k < highs), 1.0, 0.0)
            y = spec[target] / jnp.maximum(smoothed, 1.0)
            y = y.reshape(channels, windows, LANES) * inside[:, None, :]
            early = y[:, :packed_windows].reshape(packed_rows, LANES)
            late = y[:, packed_windows:].reshape(packed_rows, LANES)
            send[0, target, 0:packed_rows] = jnp.where(lower, early, pltpu.roll(late, half, 1)).astype(
                jnp.bfloat16
            )
            send[1, target, 0:packed_rows] = jnp.where(lower, pltpu.roll(early, LANES - half, 1), late).astype(
                jnp.bfloat16
            )

    def send_spec(place):
        chunk = mirrored(place, chunks)
        whiten(chunk)
        for part in range(2):
            target = 2 * chunk + part

            @pl.when(target != me)
            def _():
                spec_copy(0, me, target).start()

    send_spec(chunks - 1)

    def send_rest(step, _):
        quad = quads - 2 - step
        transform(quad, 0)
        for c in (2, 1):
            send_spec(2 * quad + c)
        return 0

    lax.fori_loop(0, quads - 1, send_rest, 0)
    send_spec(0)

    def send_later(step, _):
        spec_copy(1, me, me ^ far_near(n, step)).start()
        return 0

    lax.fori_loop(0, n - 1, send_later, 0)

    def place(source, block):
        moved[...] = block.astype(jnp.float32)
        for window in range(packed_windows):
            part = moved[pl.ds(window, channels, stride=packed_windows), :]
            swapped = pltpu.roll(part, share, 1)
            full[source, window * channels : (window + 1) * channels] = part
            turned[source, window * channels : (window + 1) * channels] = jnp.where(
                first, -swapped, swapped
            )

    def spread_flags(source, block):
        spreads = lax.dot_general(
            block, spread[...], (((0,), (0,)), ((), ())), preferred_element_type=jnp.float32
        )
        flags[source] = (
            spreads[:windows] + spreads[windows : 2 * windows] + spreads[2 * windows : 3 * windows]
        )

    flag_rows = slice(rows // 2, rows // 2 + FLAG_ROWS)
    spread_flags(me, send[0, me, flag_rows])

    def receive(part, step, _):
        source = me ^ far_near(n, step)
        spec_copy(part, source, me).wait_recv()
        if part == 0:
            spread_flags(source, recv[0, source, flag_rows])
        place(source, recv[part, source, 0:packed_rows])
        return 0

    folding = fold[me % 2]

    def order(place_index):
        return me ^ far_near(n, place_index)

    def stack_entry(entry):
        place_index = state[0]
        slot = state[1]
        reader = order(place_index % n)
        partner = partners[slot, reader]

        def window_step(window, totals):
            at = pl.multiple_of(window * channels, channels)
            straight = full[partner, pl.ds(at, channels), :]
            crossed = turned[partner, pl.ds(at, channels), :]
            totals = list(totals)
            for i in range(channels):
                own = full[reader, pl.ds(at + i, 1), :]
                totals[i] += own * straight
                totals[channels + i] += own * crossed
            return tuple(totals)

        zero = jnp.zeros((channels, LANES), jnp.float32)
        totals = lax.fori_loop(0, packed_windows, window_step, (zero,) * (2 * channels), unroll=4)
        tile = jnp.concatenate(totals, axis=0)
        high_part = tile.astype(jnp.bfloat16)
        low_part = (tile - high_part.astype(jnp.float32)).astype(jnp.bfloat16)
        flat = lax.dot_general(
            folding,
            jnp.concatenate([high_part, low_part], axis=1),
            (((1,), (1,)), ((), ())),
            preferred_element_type=jnp.float32,
        )
        common = flags[reader, :, 0:LANES] * flags[partner, :, LANES : 2 * LANES]
        common = jnp.sum(common, axis=0, keepdims=True)
        compact[entry] = (flat * (1.0 / jnp.maximum(common, 1.0))).astype(jnp.bfloat16)
        more = slot + 1 < counts[reader]
        state[0] = jnp.where(more, place_index, place_index + 1)
        state[1] = jnp.where(more, slot + 1, 0)

    entries = 2 * n
    ready = [min(slots * (p + 1), entries - (n - 1 - p)) for p in range(n)]
    added = [now - before for now, before in zip(ready, [0] + ready)]

    def send_stack(part, begin, shift, width, place_index, _):
        for extra in range(width):
            stack_entry(begin + (place_index - shift) * width + extra)
        base = state[2]
        reader = order(place_index)
        count = counts[reader]
        for slot in range(slots):
            block = compact[jnp.minimum(base + slot, entries - 1)]
            stacked[part, reader, slot] = jnp.where(slot < count, block, jnp.zeros_like(block))

        @pl.when(place_index < n - 1)
        def _():
            out_copy(part, me, reader).start()

        state[2] = base + count
        return 0

    for part in range(2):
        place(me, send[part, me, 0:packed_rows])
        lax.fori_loop(0, n - 1, functools.partial(receive, part), 0)
        for i in range(3):
            state[i] = 0
        p = 0
        while p < n:
            stop = p
            while stop < n and added[stop] == added[p]:
                stop += 1
            step = functools.partial(send_stack, part, ready[p] - added[p], p, added[p])
            lax.fori_loop(p, stop, step, 0)
            p = stop
        own_at = pl.multiple_of(me * share + part * half, half)
        out[:, pl.ds(own_at, half), :] = stacked[part, me]

    def finish_sends(step, _):
        target = peer(step)
        for part in range(2):
            spec_copy(part, me, target).wait_send()
        out_copy(0, me, target).wait_send()
        return 0

    def finish_copies(part, step, _):
        if part == 1:
            out_copy(1, me, peer(step)).wait_send()
        out_copy(part, peer(step), me).wait_recv()
        return 0

    lax.fori_loop(1, n, finish_sends, 0)
    for part in range(2):
        lax.fori_loop(1, n, functools.partial(finish_copies, part), 0)


def fused(n, records, window_valid, band_low, band_high, pair_counts, partners):
    channels, windows, length = records.shape
    bin_total = length // 2
    slots = partners.shape[1]
    share = bin_total // n
    rows = channels * windows
    table = jnp.asarray(packed_table(length, share, n))
    band = jnp.asarray(packed_band(share))
    fold = jnp.asarray(packed_fold(share))
    spread = jnp.asarray(packed_spread(channels))
    hbm = pl.BlockSpec(memory_space=pltpu.HBM)
    dma = pltpu.SemaphoreType.DMA
    by_slot = partners.T
    out = pl.pallas_call(
        functools.partial(fused_kernel, n, bin_total),
        out_shape=pltpu.VMEM((slots, bin_total, LANES), jnp.bfloat16),
        in_specs=[hbm] * 10,
        out_specs=pl.BlockSpec(memory_space=pltpu.VMEM),
        scratch_shapes=[
            pltpu.VMEM(records.shape, jnp.bfloat16),
            pltpu.VMEM(window_valid.shape, jnp.float32),
            pltpu.SMEM(band_low.shape, jnp.int32),
            pltpu.SMEM(band_high.shape, jnp.int32),
            pltpu.SMEM(pair_counts.shape, jnp.int32),
            pltpu.SMEM(by_slot.shape, jnp.int32),
            pltpu.VMEM(band.shape, jnp.bfloat16),
            pltpu.VMEM(fold.shape, jnp.bfloat16),
            pltpu.VMEM(spread.shape, jnp.bfloat16),
            pltpu.VMEM(table.shape, jnp.bfloat16),
            pltpu.VMEM((2, rows, length // 2), jnp.bfloat16),
            pltpu.VMEM((n, rows, LANES), jnp.float32),
            pltpu.VMEM((rows, (n // 2 + 2) * LANES), jnp.bfloat16),
            pltpu.VMEM((rows // 2, LANES), jnp.float32),
            pltpu.VMEM((2, n, rows // 2 + FLAG_ROWS, LANES), jnp.bfloat16),
            pltpu.VMEM((2, n, rows // 2 + FLAG_ROWS, LANES), jnp.bfloat16),
            pltpu.VMEM((n, windows, 2 * LANES), jnp.float32),
            pltpu.VMEM((n, rows // 2, LANES), jnp.float32),
            pltpu.VMEM((n, rows // 2, LANES), jnp.float32),
            pltpu.VMEM((2 * n, share // 2, LANES), jnp.bfloat16),
            pltpu.VMEM((2, n, slots, share // 2, LANES), jnp.bfloat16),
            pltpu.SMEM((3,), jnp.int32),
            dma((n // 4,)),
            dma((2, n)),
            dma((2, n)),
            dma((2, n)),
            dma((2, n)),
            dma((9,)),
        ],
        compiler_params=pltpu.CompilerParams(
            collective_id=0, has_side_effects=True, vmem_limit_bytes=60 * 1024 * 1024
        ),
    )(records, window_valid, band_low, band_high, pair_counts, by_slot, table, band, fold, spread)
    return out[None]


def solution(mesh):
    def run(records, window_valid, band_low, band_high, pair_counts, partners):
        n = mesh.shape["chan"]
        channels, windows, length = records.shape
        whole_tiles = 2 * (length // 2 // n) == LANES and 2 * channels * channels == LANES
        args = (records, window_valid, band_low, band_high, pair_counts, partners)
        if whole_tiles and n >= 8 and n & (n - 1) == 0 and windows == 32:
            return fused(n, *args)
        return body(*args)

    return jax.shard_map(
        run,
        mesh=mesh,
        in_specs=(
            P(("groups", "chan"), None, None),
            P(("groups", "chan"), None),
            P(("groups", "chan")),
            P(("groups", "chan")),
            P("groups"),
            P("groups", None),
        ),
        out_specs=P(("groups", "chan"), None, None, None),
        check_vma=False,
    )
```

```python
import functools
import math

import jax
import jax.numpy as jnp
import ml_dtypes
import numpy as np
from jax import lax
from jax.experimental import pallas as pl
from jax.experimental.pallas import tpu as pltpu
from jax.sharding import PartitionSpec as P

SMOOTH = 8


def dft_table(length, first_bin, bin_count):
    sample_index = lax.broadcasted_iota(jnp.int32, (length, bin_count), 0)
    bin_index = lax.broadcasted_iota(jnp.int32, (length, bin_count), 1) + first_bin
    phase_step = sample_index * bin_index % length
    angles = phase_step.astype(jnp.float32) * (2.0 * math.pi / length)
    return jnp.concatenate([jnp.cos(angles), -jnp.sin(angles)], axis=1).astype(jnp.bfloat16)


def finish(spectrum, band_low, band_high, channels, windows):
    bin_total = spectrum.shape[1]
    magnitude = jnp.sqrt(spectrum[0] * spectrum[0] + spectrum[1] * spectrum[1])
    padded = jnp.pad(magnitude, ((SMOOTH, SMOOTH), (0, 0)))
    summed = padded[0:bin_total]
    for offset in range(1, 2 * SMOOTH + 1):
        summed = summed + padded[offset : offset + bin_total]
    bin_column = lax.broadcasted_iota(jnp.int32, (bin_total, 1), 0)
    in_range = (
        jnp.minimum(bin_column + SMOOTH, bin_total - 1) - jnp.maximum(bin_column - SMOOTH, 0) + 1
    )
    smoothed = summed / in_range.astype(jnp.float32)
    divisor = jnp.maximum(smoothed, 1.0).reshape(bin_total, channels, windows)
    bin_index = lax.broadcasted_iota(jnp.int32, (bin_total, channels, 1), 0)
    inside = (
        (bin_index >= band_low[None, :, None]) & (bin_index < band_high[None, :, None])
    ).astype(jnp.float32)
    shaped = spectrum.reshape(2, bin_total, channels, windows)
    return (
        (shaped / divisor * inside).astype(jnp.bfloat16).reshape(2, bin_total, channels * windows)
    )


def whiten(records, window_valid, band_low, band_high):
    channels, windows, length = records.shape
    bin_total = length // 2
    row_total = channels * windows
    one_bit = (jnp.sign(records.astype(jnp.float32)) * window_valid[:, :, None]).astype(
        jnp.bfloat16
    )
    one_bit = one_bit.reshape(row_total, length)
    blocks = []
    for first_bin in range(0, bin_total, 256):
        dft_block = dft_table(length, first_bin, 256)
        partial_spec = lax.dot_general(
            dft_block, one_bit, (((0,), (1,)), ((), ())), preferred_element_type=jnp.float32
        )
        blocks.append(partial_spec.reshape(2, 256, row_total))
    spectrum = jnp.concatenate(blocks, axis=1)
    return finish(spectrum, band_low, band_high, channels, windows)


def cross_stack(first_spec, second_spec, first_flags, second_flags, in_use):
    real_part = jnp.einsum(
        "fsim,fsjm->sfij", first_spec[0], second_spec[0], preferred_element_type=jnp.float32
    )
    real_part = real_part + jnp.einsum(
        "fsim,fsjm->sfij", first_spec[1], second_spec[1], preferred_element_type=jnp.float32
    )
    imag_part = jnp.einsum(
        "fsim,fsjm->sfij", first_spec[1], second_spec[0], preferred_element_type=jnp.float32
    )
    imag_part = imag_part - jnp.einsum(
        "fsim,fsjm->sfij", first_spec[0], second_spec[1], preferred_element_type=jnp.float32
    )
    common = jnp.einsum("sim,sjm->sij", first_flags, second_flags, precision=lax.Precision.HIGHEST)
    weight = in_use[:, None, None] / jnp.maximum(common, 1.0)
    both = jnp.stack([real_part, imag_part], axis=2) * weight[:, None, None]
    return both.reshape(both.shape[0], both.shape[1], -1).astype(jnp.bfloat16)


def body(records, window_valid, band_low, band_high, pair_counts, partners):
    channels, windows, length = records.shape
    bin_total = length // 2
    readers, slot_count = partners.shape
    bin_share = bin_total // readers
    whitened = whiten(records, window_valid, band_low, band_high)
    arrived = lax.all_to_all(whitened, "chan", split_axis=1, concat_axis=2, tiled=True)
    spectra = arrived.reshape(2, bin_share, readers, channels, windows)
    copies = jnp.broadcast_to(window_valid[None], (readers, channels, windows))
    valid_all = lax.all_to_all(copies, "chan", split_axis=0, concat_axis=0, tiled=True)
    results = []
    for slot_index in range(slot_count):
        partner_ids = partners[:, slot_index]
        picks = partner_ids[:, None] == jnp.arange(readers, dtype=jnp.int32)[None, :]
        partner_spec = jnp.einsum("rq,cfqim->cfrim", picks.astype(jnp.bfloat16), spectra)
        partner_flags = jnp.einsum(
            "rq,qim->rim", picks.astype(jnp.float32), valid_all, precision=lax.Precision.HIGHEST
        )
        in_use = (slot_index < pair_counts).astype(jnp.float32)
        results.append(cross_stack(spectra, partner_spec, valid_all, partner_flags, in_use))
    stacked = jnp.stack(results, axis=1)
    return lax.all_to_all(stacked, "chan", split_axis=0, concat_axis=2, tiled=True)


LANES = 128
FLAG_ROWS = 16


def lane_bins(share):
    quarter = share // 4
    group = np.arange(LANES) % share // quarter
    start = group // 2 * 2 * quarter + 2 * (np.arange(LANES) % quarter)
    return start + group % 2, start + 1 - group % 2


def packed_table(length, share, readers):
    quarter = share // 4
    samples = np.arange(length // 2)
    tables = []
    for quad in range(readers // 4):
        for odd in range(2):
            columns = []
            for chunk in (2 * quad, 2 * quad + 1):
                order = (2 * chunk + 1, 2 * chunk) if odd else (2 * chunk, 2 * chunk + 1)
                starts = [t * share + h * share // 2 for h in range(2) for t in order]
                bins = np.concatenate([start + 2 * np.arange(quarter) + odd for start in starts])
                phase = (samples[:, None] * bins[None, :]) % length
                angles = phase.astype(np.float32) * np.float32(2.0 * math.pi / length)
                columns += [np.cos(angles), -np.sin(angles)]
            tables.append(np.concatenate(columns, axis=1))
    return np.stack(tables).reshape(readers // 4, 2, length // 2, 2 * LANES).astype(ml_dtypes.bfloat16)


def packed_band(share):
    even_first, odd_first = lane_bins(share)
    columns = np.concatenate([even_first, share + odd_first])
    front = np.arange(share) // (share // 4) % 2 == 0
    inner = np.concatenate(
        [
            np.where(front, even_first[:share], share + odd_first[:share]),
            np.where(front, share + odd_first[:share], even_first[:share]),
        ]
    )
    rows = np.concatenate([inner - LANES, inner, inner + LANES])
    near = np.abs(rows[:, None] - columns[None, :]) <= SMOOTH
    return near.astype(ml_dtypes.bfloat16)


def packed_fold(share):
    half = share // 2
    folds = []
    for order in lane_bins(share):
        placed = np.tile(order[:half], LANES // half)
        folds.append(np.arange(half)[:, None] == placed[None, :])
    return np.stack([np.concatenate([fold, fold], axis=1) for fold in folds]).astype(
        ml_dtypes.bfloat16
    )


def packed_spread(channels):
    lane = np.arange(LANES) % (channels * channels)
    rows = np.arange(channels)[:, None]
    both = np.concatenate([rows == lane // channels, rows == lane % channels], axis=1)
    unused = np.zeros((FLAG_ROWS - channels, 2 * LANES), bool)
    return np.concatenate([both, unused]).astype(ml_dtypes.bfloat16)


def fused_kernel(
    n,
    bin_total,
    records_in,
    valid_in,
    low_in,
    high_in,
    counts_in,
    partners_in,
    table,
    band_in,
    fold_in,
    spread_in,
    out,
    records,
    valid,
    low,
    high,
    counts,
    partners,
    band,
    fold,
    spread,
    tables,
    signs,
    spec,
    mags,
    moved,
    send,
    recv,
    flags,
    full,
    turned,
    compact,
    stacked,
    state,
    table_sem,
    spec_send,
    spec_recv,
    out_send,
    out_recv,
    in_sem,
):
    me = lax.axis_index("chan")
    channels, windows, length = records.shape
    share = bin_total // n
    rows = channels * windows
    slots = partners.shape[0]
    chunks = n // 2
    quads = n // 4
    samples = length // 2
    half = share // 2
    packed_windows = windows // 2
    packed_rows = rows // 2
    heights = (packed_rows + FLAG_ROWS, packed_rows)

    def far_near(count, step):
        k = step // 2
        return jnp.where(step % 2 == 0, count // 2 + (k ^ 2), count // 2 - 1 - k)

    def peer(step):
        return me ^ step

    barrier = pltpu.get_barrier_semaphore()
    def table_copy(quad):
        return pltpu.make_async_copy(table.at[quad], tables.at[quad], table_sem.at[quad])

    inputs = [
        pltpu.make_async_copy(source, target, in_sem.at[i])
        for i, (source, target) in enumerate(
            [
                (valid_in, valid),
                (records_in, records),
                (low_in, low),
                (high_in, high),
                (counts_in, counts),
                (partners_in, partners),
                (band_in, band),
                (fold_in, fold),
                (spread_in, spread),
            ]
        )
    ]
    for copy in inputs:
        copy.start()
    for place in reversed(range(quads)):
        table_copy(place + me // (n // 2) * (quads - 1 - 2 * place)).start()
    for step in range(1, n):
        pl.semaphore_signal(
            barrier, inc=1, device_id={"chan": peer(step)}, device_id_type=pl.DeviceIdType.MESH
        )
    inputs[0].wait()

    pieces = []
    rest = valid[...]
    for _ in range(3):
        piece = rest.astype(jnp.bfloat16).astype(jnp.float32)
        rest = rest - piece
        pieces.append(piece)
    unused = jnp.zeros((channels, LANES - 3 * windows), jnp.float32)
    pieces = jnp.concatenate(pieces + [unused], axis=1)
    pieces = jnp.concatenate([pieces, jnp.zeros((FLAG_ROWS - channels, LANES), jnp.float32)], axis=0)
    for target in range(n):
        send[0, target, rows // 2 : rows // 2 + FLAG_ROWS] = pieces.astype(jnp.bfloat16)

    row = lax.broadcasted_iota(jnp.int32, (rows, windows), 0)
    window_lane = lax.broadcasted_iota(jnp.int32, (rows, windows), 1)
    spread_valid = jnp.broadcast_to(valid[...][:, None, :], (channels, windows, windows))
    spread_valid = spread_valid.reshape(rows, windows)
    level = jnp.sum(
        jnp.where(row % windows == window_lane, spread_valid, 0.0), axis=1, keepdims=True
    )
    level = jnp.broadcast_to(level, (rows, LANES)).astype(jnp.bfloat16)

    inputs[1].wait()

    def to_signs(part, _):
        at = pl.multiple_of(part * LANES, LANES)
        later = pl.multiple_of(samples + part * LANES, LANES)

        def sign(x):
            one = jnp.ones_like(x)
            return jnp.where(x > 0, one, jnp.where(x < 0, -one, jnp.zeros_like(x)))

        a = sign(records[:, :, pl.ds(at, LANES)].reshape(rows, LANES))
        b = sign(records[:, :, pl.ds(later, LANES)].reshape(rows, LANES))
        signs[0, :, pl.ds(at, LANES)] = (a + b) * level
        signs[1, :, pl.ds(at, LANES)] = (a - b) * level
        return 0

    lax.fori_loop(0, samples // LANES, to_signs, 0)
    for copy in inputs[2:]:
        copy.wait()

    lane = lax.broadcasted_iota(jnp.int32, (1, LANES), 1)
    first = lane < share
    inner = lane % share
    quarter = share // 4
    front = inner // quarter % 2 == 0
    lower = inner < half

    mags[:, 0:LANES] = jnp.zeros((rows, LANES), jnp.bfloat16)
    mags[:, (chunks + 1) * LANES : (chunks + 2) * LANES] = jnp.zeros((rows, LANES), jnp.bfloat16)

    upper = me // (n // 2)

    def mirrored(place, count):
        return place + upper * (count - 1 - 2 * place)

    def transform(place, _):
        quad = mirrored(place, quads)
        table_copy(quad).wait()
        even = jnp.dot(signs[0], tables[quad, 0], preferred_element_type=jnp.float32)
        odd = jnp.dot(signs[1], tables[quad, 1], preferred_element_type=jnp.float32)
        for part in range(2):
            chunk = 2 * quad + part
            e = even[:, part * LANES : (part + 1) * LANES]
            o = odd[:, part * LANES : (part + 1) * LANES]
            spec[2 * chunk] = jnp.where(front, e, o)
            spec[2 * chunk + 1] = jnp.where(front, o, e)
            e, o = e * e, o * o
            e, o = e + pltpu.roll(e, share, 1), o + pltpu.roll(o, share, 1)
            at = pl.multiple_of((chunk + 1) * LANES, LANES)
            mags[:, pl.ds(at, LANES)] = jnp.sqrt(jnp.where(first, e, o)).astype(jnp.bfloat16)
        return 0

    transform(quads - 1, 0)


    def spec_copy(part, source, target):
        return pltpu.make_async_remote_copy(
            src_ref=send.at[part, target, pl.ds(0, heights[part])],
            dst_ref=recv.at[part, source, pl.ds(0, heights[part])],
            send_sem=spec_send.at[part, target],
            recv_sem=spec_recv.at[part, source],
            device_id={"chan": target},
            device_id_type=pl.DeviceIdType.MESH,
        )

    def out_copy(part, source, target):
        at = pl.multiple_of(source * share + part * half, half)
        return pltpu.make_async_remote_copy(
            src_ref=stacked.at[part, target],
            dst_ref=out.at[:, pl.ds(at, half), :],
            send_sem=out_send.at[part, target],
            recv_sem=out_recv.at[part, source],
            device_id={"chan": target},
            device_id_type=pl.DeviceIdType.MESH,
        )

    channel = lax.broadcasted_iota(jnp.int32, (channels, 1), 0)
    lows = jnp.zeros((channels, 1), jnp.int32)
    highs = jnp.zeros((channels, 1), jnp.int32)
    for c in range(channels):
        lows = jnp.where(channel == c, low[c], lows)
        highs = jnp.where(channel == c, high[c], highs)

    def whiten(chunk):
        at = pl.multiple_of(chunk * LANES, LANES)
        total = jnp.dot(
            mags[:, pl.ds(at, 3 * LANES)], band[...], preferred_element_type=jnp.float32
        )
        for part in range(2):
            target = 2 * chunk + part
            k = target * share + inner // half * half + 2 * (inner % quarter)
            k = k + jnp.where(front, part, 1 - part)
            near = jnp.minimum(k + SMOOTH, bin_total - 1) - jnp.maximum(k - SMOOTH, 0) + 1
            smoothed = total[:, part * LANES : (part + 1) * LANES] * (1.0 / near.astype(jnp.float32))
            inside = jnp.where((k >= lows) & (k < highs), 1.0, 0.0)
            y = spec[target] / jnp.maximum(smoothed, 1.0)
            y = y.reshape(channels, windows, LANES) * inside[:, None, :]
            early = y[:, :packed_windows].reshape(packed_rows, LANES)
            late = y[:, packed_windows:].reshape(packed_rows, LANES)
            send[0, target, 0:packed_rows] = jnp.where(lower, early, pltpu.roll(late, half, 1)).astype(
                jnp.bfloat16
            )
            send[1, target, 0:packed_rows] = jnp.where(lower, pltpu.roll(early, LANES - half, 1), late).astype(
                jnp.bfloat16
            )

    def send_spec(place):
        chunk = mirrored(chunks - 1 if place is None else place, chunks)
        if place is not None:
            whiten(chunk)
        for part in range(2):
            target = 2 * chunk + part

            @pl.when(target != me)
            def _():
                spec_copy(0, me, target).start()

    whiten(mirrored(chunks - 1, chunks))
    pl.semaphore_wait(barrier, n - 1)
    send_spec(None)

    def send_rest(step, _):
        quad = quads - 2 - step
        transform(quad, 0)
        for c in (2, 1):
            send_spec(2 * quad + c)
        return 0

    lax.fori_loop(0, quads - 1, send_rest, 0)
    send_spec(0)

    def send_later(step, _):
        spec_copy(1, me, me ^ far_near(n, step)).start()
        return 0

    lax.fori_loop(0, n - 1, send_later, 0)

    def place(source, block):
        moved[...] = block.astype(jnp.float32)
        for window in range(packed_windows):
            part = moved[pl.ds(window, channels, stride=packed_windows), :]
            swapped = pltpu.roll(part, share, 1)
            full[source, window * channels : (window + 1) * channels] = part
            turned[source, window * channels : (window + 1) * channels] = jnp.where(
                first, -swapped, swapped
            )

    def spread_flags(source, block):
        spreads = lax.dot_general(
            block, spread[...], (((0,), (0,)), ((), ())), preferred_element_type=jnp.float32
        )
        flags[source] = (
            spreads[:windows] + spreads[windows : 2 * windows] + spreads[2 * windows : 3 * windows]
        )

    flag_rows = slice(rows // 2, rows // 2 + FLAG_ROWS)
    spread_flags(me, send[0, me, flag_rows])

    def receive(part, step, _):
        source = me ^ far_near(n, step)
        spec_copy(part, source, me).wait_recv()
        if part == 0:
            spread_flags(source, recv[0, source, flag_rows])
        place(source, recv[part, source, 0:packed_rows])
        return 0

    folding = fold[me % 2]

    def order(place_index):
        return me ^ far_near(n, place_index)

    def stack_entry(entry):
        place_index = state[0]
        slot = state[1]
        reader = order(place_index % n)
        partner = partners[slot, reader]

        def window_step(window, totals):
            at = pl.multiple_of(window * channels, channels)
            straight = full[partner, pl.ds(at, channels), :]
            crossed = turned[partner, pl.ds(at, channels), :]
            totals = list(totals)
            for i in range(channels):
                own = full[reader, pl.ds(at + i, 1), :]
                totals[i] += own * straight
                totals[channels + i] += own * crossed
            return tuple(totals)

        zero = jnp.zeros((channels, LANES), jnp.float32)
        totals = lax.fori_loop(0, packed_windows, window_step, (zero,) * (2 * channels), unroll=4)
        tile = jnp.concatenate(totals, axis=0)
        high_part = tile.astype(jnp.bfloat16)
        low_part = (tile - high_part.astype(jnp.float32)).astype(jnp.bfloat16)
        flat = lax.dot_general(
            folding,
            jnp.concatenate([high_part, low_part], axis=1),
            (((1,), (1,)), ((), ())),
            preferred_element_type=jnp.float32,
        )
        common = flags[reader, :, 0:LANES] * flags[partner, :, LANES : 2 * LANES]
        common = jnp.sum(common, axis=0, keepdims=True)
        compact[entry] = (flat * (1.0 / jnp.maximum(common, 1.0))).astype(jnp.bfloat16)
        more = slot + 1 < counts[reader]
        state[0] = jnp.where(more, place_index, place_index + 1)
        state[1] = jnp.where(more, slot + 1, 0)

    entries = 2 * n
    ready = [min(slots * (p + 1), entries - (n - 1 - p)) for p in range(n)]
    added = [now - before for now, before in zip(ready, [0] + ready)]

    def send_stack(part, begin, shift, width, place_index, _):
        for extra in range(width):
            stack_entry(begin + (place_index - shift) * width + extra)
        base = state[2]
        reader = order(place_index)
        count = counts[reader]
        for slot in range(slots):
            block = compact[jnp.minimum(base + slot, entries - 1)]
            stacked[part, reader, slot] = jnp.where(slot < count, block, jnp.zeros_like(block))

        @pl.when(place_index < n - 1)
        def _():
            out_copy(part, me, reader).start()

        state[2] = base + count
        return 0

    for part in range(2):
        place(me, send[part, me, 0:packed_rows])
        lax.fori_loop(0, n - 1, functools.partial(receive, part), 0)
        for i in range(3):
            state[i] = 0
        p = 0
        while p < n:
            stop = p
            while stop < n and added[stop] == added[p]:
                stop += 1
            step = functools.partial(send_stack, part, ready[p] - added[p], p, added[p])
            lax.fori_loop(p, stop, step, 0)
            p = stop
        own_at = pl.multiple_of(me * share + part * half, half)
        out[:, pl.ds(own_at, half), :] = stacked[part, me]

    def finish_sends(step, _):
        target = peer(step)
        for part in range(2):
            spec_copy(part, me, target).wait_send()
        out_copy(0, me, target).wait_send()
        return 0

    def finish_copies(part, step, _):
        if part == 1:
            out_copy(1, me, peer(step)).wait_send()
        out_copy(part, peer(step), me).wait_recv()
        return 0

    lax.fori_loop(1, n, finish_sends, 0)
    for part in range(2):
        lax.fori_loop(1, n, functools.partial(finish_copies, part), 0)


def fused(n, records, window_valid, band_low, band_high, pair_counts, partners):
    channels, windows, length = records.shape
    bin_total = length // 2
    slots = partners.shape[1]
    share = bin_total // n
    rows = channels * windows
    table = jnp.asarray(packed_table(length, share, n))
    band = jnp.asarray(packed_band(share))
    fold = jnp.asarray(packed_fold(share))
    spread = jnp.asarray(packed_spread(channels))
    hbm = pl.BlockSpec(memory_space=pltpu.HBM)
    dma = pltpu.SemaphoreType.DMA
    by_slot = partners.T
    out = pl.pallas_call(
        functools.partial(fused_kernel, n, bin_total),
        out_shape=pltpu.VMEM((slots, bin_total, LANES), jnp.bfloat16),
        in_specs=[hbm] * 10,
        out_specs=pl.BlockSpec(memory_space=pltpu.VMEM),
        scratch_shapes=[
            pltpu.VMEM(records.shape, jnp.bfloat16),
            pltpu.VMEM(window_valid.shape, jnp.float32),
            pltpu.SMEM(band_low.shape, jnp.int32),
            pltpu.SMEM(band_high.shape, jnp.int32),
            pltpu.SMEM(pair_counts.shape, jnp.int32),
            pltpu.SMEM(by_slot.shape, jnp.int32),
            pltpu.VMEM(band.shape, jnp.bfloat16),
            pltpu.VMEM(fold.shape, jnp.bfloat16),
            pltpu.VMEM(spread.shape, jnp.bfloat16),
            pltpu.VMEM(table.shape, jnp.bfloat16),
            pltpu.VMEM((2, rows, length // 2), jnp.bfloat16),
            pltpu.VMEM((n, rows, LANES), jnp.float32),
            pltpu.VMEM((rows, (n // 2 + 2) * LANES), jnp.bfloat16),
            pltpu.VMEM((rows // 2, LANES), jnp.float32),
            pltpu.VMEM((2, n, rows // 2 + FLAG_ROWS, LANES), jnp.bfloat16),
            pltpu.VMEM((2, n, rows // 2 + FLAG_ROWS, LANES), jnp.bfloat16),
            pltpu.VMEM((n, windows, 2 * LANES), jnp.float32),
            pltpu.VMEM((n, rows // 2, LANES), jnp.float32),
            pltpu.VMEM((n, rows // 2, LANES), jnp.float32),
            pltpu.VMEM((2 * n, share // 2, LANES), jnp.bfloat16),
            pltpu.VMEM((2, n, slots, share // 2, LANES), jnp.bfloat16),
            pltpu.SMEM((3,), jnp.int32),
            dma((n // 4,)),
            dma((2, n)),
            dma((2, n)),
            dma((2, n)),
            dma((2, n)),
            dma((9,)),
        ],
        compiler_params=pltpu.CompilerParams(
            collective_id=0, has_side_effects=True, vmem_limit_bytes=60 * 1024 * 1024
        ),
    )(records, window_valid, band_low, band_high, pair_counts, by_slot, table, band, fold, spread)
    return out[None]


def solution(mesh):
    def run(records, window_valid, band_low, band_high, pair_counts, partners):
        n = mesh.shape["chan"]
        channels, windows, length = records.shape
        whole_tiles = 2 * (length // 2 // n) == LANES and 2 * channels * channels == LANES
        args = (records, window_valid, band_low, band_high, pair_counts, partners)
        if whole_tiles and n >= 8 and n & (n - 1) == 0 and windows == 32:
            return fused(n, *args)
        return body(*args)

    return jax.shard_map(
        run,
        mesh=mesh,
        in_specs=(
            P(("groups", "chan"), None, None),
            P(("groups", "chan"), None),
            P(("groups", "chan")),
            P(("groups", "chan")),
            P("groups"),
            P("groups", None),
        ),
        out_specs=P(("groups", "chan"), None, None, None),
        check_vma=False,
    )
```
